128 devices in a mesh: replica: 16 (over y, x_lo, core), fsdp: 8 (over x_hi, z).
Axes of the slice: x: 4 (x_hi: 2, x_lo: 2; x = x_hi * 2 + x_lo), y: 4, z: 4, core: 2. Of those that a mesh axis runs over, the one named last changes fastest.
Arguments:
- tokens: bfloat16 [16384, 4096], P(('replica', 'fsdp')), may hold values from -6 to 6
- out_grads: bfloat16 [16384, 14336], P(('replica', 'fsdp')), may hold values from -0.1875 to 0.1875
- block_ids: int32 [8], replicated, may hold values from 0 to 55, as said below
- left_basis: bfloat16 [16, 8, 1024, 1024], P('replica', 'fsdp'), may hold values from -0.1875 to 0.1875
- right_basis: bfloat16 [16, 8, 1024, 1024], P('replica', 'fsdp'), may hold values from -0.1875 to 0.1875
- first_moment: bfloat16 [16, 8, 1024, 1024], P('replica', 'fsdp'), may hold values from -3 to 3
- second_moment: bfloat16 [16, 8, 1024, 1024], P('replica', 'fsdp'), may hold values from 0.0099487305 to 1
- outer_params: float32 [1024, 8192], P('fsdp'), may hold values from -6 to 6
- outer_momentum: float32 [1024, 8192], P('fsdp'), may hold values from -3 to 3
- snapshot: bfloat16 [16, 1024, 8192], P('replica', 'fsdp'), may hold values from -6 to 6
- local_params: bfloat16 [16, 1024, 8192], P('replica', 'fsdp'), may hold values from -6 to 6
- due_rows: int32 [1024], P('fsdp'), may hold values 0 or 1
Outputs:
- update: bfloat16 [16, 8, 1024, 1024], P('replica', 'fsdp')
- first_next: bfloat16 [16, 8, 1024, 1024], P('replica', 'fsdp')
- second_next: bfloat16 [16, 8, 1024, 1024], P('replica', 'fsdp')
- outer_next: float32 [1024, 8192], P('fsdp')
- momentum_next: float32 [1024, 8192], P('fsdp')
- local_next: bfloat16 [16, 1024, 8192], P('replica', 'fsdp')
The draws below stay inside these ranges and needn't reach their ends.
Inputs may be any that keep to these rules, and one draw needn't show every extreme that they name: `block_ids`: 8 different block numbers of the window; slot s belongs to fsdp index s.
All inputs are finite; a program needn't handle non-finite values. No bound on the sum of `due_rows` on one device may be relied on, other than what follows from the above.
Results may differ from the reference program's by a relative error of at most 0.022.
Values may be sent and summed in bfloat16 or wider, within the bound.
No kernel may reach another device: no remote copies, remote signals or barrier semaphores. Data moves between devices by JAX's collectives and lax.ppermute only.
A program may use at most 192 MiB of HBM per device.

```python
import math
import jax
import jax.numpy as jnp
from jax import lax

D = 8192
DW = 4096
FW = 14336
BLOCK = 1024
TOK_DEV = 128
GRID = 56
NBLK = 8
TOKENS = 16384
FRAG_ROWS = 1024
REPLICAS = 16
N_REPLICA = 16
N_FSDP = 8


def draw_block_ids(key, part):
    key = jax.random.fold_in(key, 11)
    first_key, second_key = jax.random.split(key)
    middle = jax.random.permutation(first_key, GRID - 2) + 1
    chosen = jnp.concatenate([jnp.array([0, GRID - 1], jnp.int32), middle[:NBLK - 2].astype(jnp.int32)])
    return jax.random.permutation(second_key, chosen).astype(jnp.int32)


def with_ends(entries, key, smallest, largest):
    longest = entries.shape.index(max(entries.shape))
    spots = []
    for shift in (0, 1):
        where = [jax.random.randint(jax.random.fold_in(key, axis), (), 0, length) for axis, length in enumerate(entries.shape)]
        where[longest] = (where[longest] + shift) % entries.shape[longest]
        spots.append(tuple(where))
    return entries.at[spots[0]].set(smallest).at[spots[1]].set(largest)


def steps_of(key, extent, shards, low, high):
    gain = 1.0
    for dim, blocks in shards:
        steps = jax.random.uniform(jax.random.fold_in(jax.random.fold_in(key, 6), dim), (blocks,), jnp.float32, low / len(shards), high / len(shards))
        gain = gain * jnp.repeat(jnp.exp(steps), extent[dim] // blocks).reshape((-1,) + (1,) * (len(extent) - 1 - dim))
    return gain


def scatter_about(stream_key, shape, width, most, cuts=(), kind=jnp.bfloat16):
    loudness = steps_of(stream_key, shape, cuts, -0.22, 0.18) if cuts else 1.0
    values = jax.random.normal(stream_key, shape, jnp.float32) * width * loudness
    return jnp.minimum(jnp.maximum(values, -most), most).astype(kind)


def setup_inputs(seed: int = 0) -> dict:
    splits = jax.random.split(jax.random.key(seed), 13)
    tokens = scatter_about(splits[0], (TOKENS, DW), 1.0, 6.0, ((0, 128),))
    out_grads = scatter_about(splits[1], (TOKENS, FW), (TOK_DEV * N_FSDP) ** -0.5, 0.1875, ((0, 128),))
    block_ids = draw_block_ids(jax.random.fold_in(splits[12], 71), 0)
    left_basis = scatter_about(splits[3], (REPLICAS, NBLK, BLOCK, BLOCK), BLOCK ** -0.5, 0.1875, ((0, 16), (1, 8)))
    right_basis = scatter_about(splits[4], (REPLICAS, NBLK, BLOCK, BLOCK), BLOCK ** -0.5, 0.1875, ((0, 16), (1, 8)))
    first_moment = scatter_about(splits[5], (REPLICAS, NBLK, BLOCK, BLOCK), 0.5, 3.0, ((0, 16), (1, 8)))
    second_moment = jnp.clip(jnp.exp(math.log(1.0) - 4.61031033 * jax.random.uniform(splits[6], (REPLICAS, NBLK, BLOCK, BLOCK), jnp.float32) ** steps_of(splits[6], (REPLICAS, NBLK, BLOCK, BLOCK), ((0, 16), (1, 8)), -0.2, 0.2)), 0.0099487305, 1.0).astype(jnp.bfloat16)
    outer_params = scatter_about(splits[7], (FRAG_ROWS, D), 1.0, 6.0, ((0, 8),), jnp.float32)
    outer_momentum = scatter_about(splits[8], (FRAG_ROWS, D), 0.5, 3.0, ((0, 8),), jnp.float32)
    snapshot = scatter_about(splits[9], (REPLICAS, FRAG_ROWS, D), 1.0, 6.0, ((0, 16), (1, 8)))
    local_params = scatter_about(splits[10], (REPLICAS, FRAG_ROWS, D), 1.0, 6.0, ((0, 16), (1, 8)))
    due_rows = with_ends((jax.random.randint(splits[11], (FRAG_ROWS,), 0, 2) < 1).astype(jnp.int32), jax.random.fold_in(splits[11], 1), 0, 1)
    return dict(tokens=tokens, out_grads=out_grads, block_ids=block_ids, left_basis=left_basis, right_basis=right_basis, first_moment=first_moment, second_moment=second_moment, outer_params=outer_params, outer_momentum=outer_momentum, snapshot=snapshot, local_params=local_params, due_rows=due_rows)


def soap_block(grad, left, right, first, second):
    half = jnp.dot(left.T, grad, preferred_element_type=jnp.float32).astype(jnp.bfloat16)
    rotated = jnp.dot(half, right, preferred_element_type=jnp.float32)
    moment_one = 0.95 * first.astype(jnp.float32) + 0.05 * rotated
    moment_two = 0.95 * second.astype(jnp.float32) + 0.05 * rotated * rotated
    correct = 1.0 - 0.95 ** 10
    direction = (moment_one / correct / (jnp.sqrt(moment_two / correct) + 1e-08)).astype(jnp.bfloat16)
    back = jnp.dot(left, direction, preferred_element_type=jnp.float32).astype(jnp.bfloat16)
    update = jnp.dot(back, right.T, preferred_element_type=jnp.float32).astype(jnp.bfloat16)
    return (update, moment_one.astype(jnp.bfloat16), moment_two.astype(jnp.bfloat16))

def reference(tokens, out_grads, block_ids, left_basis, right_basis, first_moment, second_moment, outer_params, outer_momentum, snapshot, local_params, due_rows):
    columns = FW // BLOCK
    inputs = tokens.reshape(N_REPLICA, N_FSDP, TOK_DEV, DW)
    grads_out = out_grads.reshape(N_REPLICA, N_FSDP, TOK_DEV, FW)

    def one_replica(items):
        xin, dout, lefts, rights, firsts, seconds = items

        def one_block(entry):
            block, left, right, first, second = entry
            row_start = block // columns * BLOCK
            col_start = block % columns * BLOCK
            xcols = lax.dynamic_slice_in_dim(xin, row_start, BLOCK, 2).astype(jnp.float32)
            dcols = lax.dynamic_slice_in_dim(dout, col_start, BLOCK, 2).astype(jnp.float32)
            parts = jnp.einsum('fti,ftj->fij', xcols, dcols)
            parts = lax.optimization_barrier(parts.astype(jnp.bfloat16)).astype(jnp.float32)
            grad = lax.optimization_barrier(jnp.sum(parts, axis=0)).astype(jnp.bfloat16)
            return soap_block(grad, left, right, first, second)
        return lax.map(one_block, (block_ids, lefts, rights, firsts, seconds))
    update, first_next, second_next = lax.map(one_replica, (inputs, grads_out, left_basis, right_basis, first_moment, second_moment))
    snap = snapshot.astype(jnp.float32)
    pseudo = lax.optimization_barrier(jnp.sum(outer_params[None] - snap, axis=0)) / N_REPLICA
    moment = 0.9 * outer_momentum + pseudo
    stepped = outer_params - 0.7 * (pseudo + 0.9 * moment)
    due = (due_rows == 1)[:, None]
    outer_next = jnp.where(due, stepped, outer_params)
    momentum_next = jnp.where(due, moment, outer_momentum)
    merged = (stepped[None] + (local_params.astype(jnp.float32) - snap)).astype(jnp.bfloat16)
    local_next = jnp.where(due[None], merged, local_params)
    return (update, first_next, second_next, outer_next, momentum_next, local_next)
```

```python
import jax
import jax.numpy as jnp
from jax import lax
from jax.sharding import PartitionSpec as P

FW = 14336
BLOCK = 1024
AXES = ("replica", "fsdp")
SHIFTS = ((1, 2), (1, 1), (1, 3), (0, 2), (1, 0), (0, 1), (0, 3))


def place(index):
    replica, fsdp = divmod(index, 8)
    return replica // 4, replica // 2 % 2, replica % 2, fsdp // 4, fsdp % 4


def index_of(y, x_lo, core, x_hi, z):
    return ((y % 4 * 2 + x_lo % 2) * 2 + core % 2) * 8 + x_hi % 2 * 4 + z % 4


def moved(array, y=0, x_lo=0, core=0, x_hi=0, z=0):
    pairs = []
    for source in range(128):
        at = place(source)
        pairs.append((source, index_of(at[0] + y, at[1] + x_lo, at[2] + core, at[3] + x_hi, at[4] + z)))
    return lax.ppermute(array, AXES, pairs)


def per_device(
    tokens,
    out_grads,
    block_ids,
    left_basis,
    right_basis,
    first_moment,
    second_moment,
    outer_params,
    outer_momentum,
    snapshot,
    local_params,
    due_rows,
):
    columns = FW // BLOCK
    me = lax.axis_index("fsdp")
    x_hi, z = me // 4, me % 4
    replica = lax.axis_index("replica")
    y, core = replica // 4, replica % 2

    def factors(owner):
        block = block_ids[owner]
        xcols = lax.dynamic_slice_in_dim(tokens, block // columns * BLOCK, BLOCK, 1)
        dcols = lax.dynamic_slice_in_dim(out_grads, block % columns * BLOCK, BLOCK, 1)
        return jnp.concatenate([xcols, dcols], axis=1)

    got = []
    for dx, dz in SHIFTS:
        owner = (x_hi + dx) % 2 * 4 + (z + dz) % 4
        got.append(moved(factors(owner), x_hi=dx, z=dz))
    got.append(factors(me))
    both = jnp.concatenate(got, axis=0)
    grad = lax.dot_general(
        both[:, :BLOCK], both[:, BLOCK:], (((0,), (0,)), ((), ())), preferred_element_type=jnp.float32
    ).astype(jnp.bfloat16)
    left = left_basis[0, 0]
    right = right_basis[0, 0]
    f32 = jnp.float32
    half = lax.dot_general(left, grad, (((0,), (0,)), ((), ())), preferred_element_type=f32).astype(jnp.bfloat16)
    rotated = jnp.dot(half, right, preferred_element_type=f32)
    moment_one = 0.95 * first_moment[0, 0].astype(f32) + 0.05 * rotated
    moment_two = 0.95 * second_moment[0, 0].astype(f32) + 0.05 * rotated * rotated
    correct = 1.0 - 0.95**10
    direction = (moment_one / correct / (jnp.sqrt(moment_two / correct) + 1e-08)).astype(jnp.bfloat16)
    back = jnp.dot(left, direction, preferred_element_type=f32).astype(jnp.bfloat16)
    update = lax.dot_general(back, right, (((1,), (1,)), ((), ())), preferred_element_type=f32).astype(jnp.bfloat16)

    snap = snapshot[0].astype(f32)
    diff = (outer_params - snap).astype(jnp.bfloat16).reshape(2, 4, 16, 8192)
    other = moved(lax.dynamic_index_in_dim(diff, 1 - core, 0, False), core=1)
    pair = (lax.dynamic_index_in_dim(diff, core, 0, False).astype(f32) + other.astype(f32)).astype(jnp.bfloat16)
    parts = [lax.dynamic_index_in_dim(pair, y, 0, False)]
    for dy in (1, 2, 3):
        parts.append(moved(lax.dynamic_index_in_dim(pair, (y + dy) % 4, 0, False), y=dy))
    plane = sum(p.astype(f32) for p in parts).astype(jnp.bfloat16)
    total = (plane.astype(f32) + moved(plane, x_lo=1).astype(f32)).astype(jnp.bfloat16)
    rows = jnp.zeros((4, 16, 8192), jnp.bfloat16)
    rows = lax.dynamic_update_index_in_dim(rows, total, y, 0)
    for dy in (1, 2, 3):
        rows = lax.dynamic_update_index_in_dim(rows, moved(total, y=dy), (y - dy) % 4, 0)
    other = moved(rows, core=1)
    whole = jnp.where(core == 0, jnp.stack([rows, other]), jnp.stack([other, rows])).reshape(128, 8192)
    pseudo = whole.astype(f32) / lax.axis_size("replica")
    moment = 0.9 * outer_momentum + pseudo
    stepped = outer_params - 0.7 * (pseudo + 0.9 * moment)
    due = (due_rows == 1)[:, None]
    outer_next = jnp.where(due, stepped, outer_params)
    momentum_next = jnp.where(due, moment, outer_momentum)
    merged = (stepped + (local_params[0].astype(f32) - snap)).astype(jnp.bfloat16)
    local_next = jnp.where(due, merged, local_params[0])
    return (
        update[None, None],
        moment_one.astype(jnp.bfloat16)[None, None],
        moment_two.astype(jnp.bfloat16)[None, None],
        outer_next,
        momentum_next,
        local_next[None],
    )


def solution(mesh):
    return jax.shard_map(
        per_device,
        mesh=mesh,
        in_specs=(
            P(("replica", "fsdp"), None),
            P(("replica", "fsdp"), None),
            P(),
            P("replica", "fsdp", None, None),
            P("replica", "fsdp", None, None),
            P("replica", "fsdp", None, None),
            P("replica", "fsdp", None, None),
            P("fsdp", None),
            P("fsdp", None),
            P("replica", "fsdp", None),
            P("replica", "fsdp", None),
            P("fsdp"),
        ),
        out_specs=(
            P("replica", "fsdp", None, None),
            P("replica", "fsdp", None, None),
            P("replica", "fsdp", None, None),
            P("fsdp", None),
            P("fsdp", None),
            P("replica", "fsdp", None),
        ),
        check_vma=False,
    )
```

```python
import functools

import jax
import jax.numpy as jnp
from jax import lax
from jax.experimental import pallas as pl
from jax.experimental.pallas import tpu as pltpu
from jax.sharding import PartitionSpec as P

FW = 14336
BLOCK = 1024
TOK = 128
AXES = ("replica", "fsdp")
SHIFTS = ((1, 2), (1, 1), (1, 3), (0, 2), (1, 0), (0, 1), (0, 3))
EARLY = 5
CORRECT = 1.0 - 0.95**10
F32 = jnp.float32
BF16 = jnp.bfloat16
VM = pl.BlockSpec(memory_space=pltpu.VMEM)
ANY = pl.BlockSpec(memory_space=pl.ANY)


def place(index):
    replica, fsdp = divmod(index, 8)
    return replica // 4, replica // 2 % 2, replica % 2, fsdp // 4, fsdp % 4


def index_of(y, x_lo, core, x_hi, z):
    return ((y % 4 * 2 + x_lo % 2) * 2 + core % 2) * 8 + x_hi % 2 * 4 + z % 4


def moved(array, where):
    return lax.ppermute(array, AXES, [(s, index_of(*where(*place(s)))) for s in range(128)])


def to_owner(array, dx, dz):
    return moved(array, lambda y, x_lo, core, x_hi, z: (y, x_lo, core, x_hi + dx, z + dz))


def to_core(array):
    return moved(array, lambda y, x_lo, core, x_hi, z: (y, x_lo, core + 1, x_hi, z))


def to_x(array):
    return moved(array, lambda y, x_lo, core, x_hi, z: (y, x_lo + 1, core, x_hi, z))


def to_y(array, flips):
    return moved(array, lambda y, x_lo, core, x_hi, z: (y ^ flips[core], x_lo, core, x_hi, z))


def vmem(array):
    return pltpu.with_memory_space_constraint(array, pltpu.VMEM)


def hbm(array):
    return pltpu.with_memory_space_constraint(array, pltpu.HBM)


def pick_kernel(ids, tokens, out_grads, *rest):
    outs, (held, sems, out_sems) = rest[:-3], rest[-3:]
    columns = FW // BLOCK
    me = lax.axis_index("fsdp")
    x_hi, z = me // 4, me % 4
    copies = []
    for i, (dx, dz) in enumerate(SHIFTS + ((0, 0),)):
        owner = (x_hi + dx) % 2 * 4 + (z + dz) % 4
        block = ids[owner]
        row = pl.multiple_of(block // columns * BLOCK, BLOCK)
        col = pl.multiple_of(block % columns * BLOCK, BLOCK)
        for k, (source, at) in enumerate(((tokens, row), (out_grads, col))):
            copy = pltpu.make_async_copy(
                source.at[:, pl.ds(at, BLOCK)], held.at[i, :, pl.ds(k * BLOCK, BLOCK)], sems.at[2 * i + k]
            )
            copy.start()
            copies.append(copy)
    stores = []
    for i, out in enumerate(outs):
        copies[2 * i].wait()
        copies[2 * i + 1].wait()
        store = pltpu.make_async_copy(held.at[i], out, out_sems.at[i])
        store.start()
        stores.append(store)
    for store in stores:
        store.wait()


def pick(block_ids, tokens, out_grads):
    n = len(SHIFTS) + 1
    return pl.pallas_call(
        pick_kernel,
        out_shape=[pltpu.HBM((TOK, 2 * BLOCK), BF16)] * n,
        in_specs=[pl.BlockSpec(memory_space=pltpu.SMEM), ANY, ANY],
        out_specs=[ANY] * n,
        scratch_shapes=[
            pltpu.VMEM((n, TOK, 2 * BLOCK), BF16),
            pltpu.SemaphoreType.DMA((2 * n,)),
            pltpu.SemaphoreType.DMA((n,)),
        ],
        compiler_params=pltpu.CompilerParams(vmem_limit_bytes=6 << 20),
        cost_estimate=pl.CostEstimate(flops=0, bytes_accessed=8 << 20, transcendentals=0),
        name="pick",
    )(block_ids, hbm(tokens), hbm(out_grads))


def rotate(bufs, left, right, yt, zz):
    step = 256

    @pl.loop(0, BLOCK // step)
    def _(j):
        at = pl.ds(pl.multiple_of(j * step, step), step)
        xs = jnp.concatenate([b[:, :BLOCK] for b in bufs], axis=0)
        ds = jnp.concatenate([b[:, BLOCK:] for b in bufs], axis=0)
        yt[at, :] = jnp.dot(xs, left[:, at], preferred_element_type=F32).T.astype(BF16)
        zz[:, at] = jnp.dot(ds, right[:, at], preferred_element_type=F32).astype(BF16)


def early_kernel(n, *refs):
    sources, (left, right, acc, yt, zz, bufs, sems) = refs[:n], refs[n:]
    copies = [pltpu.make_async_copy(source, bufs.at[i], sems.at[i]) for i, source in enumerate(sources)]
    for copy in copies:
        copy.start()
    for copy in copies:
        copy.wait()
    bufs = [bufs.at[i] for i in range(n)]
    rotate(bufs, left, right, yt, zz)

    @pl.loop(0, 4)
    def _(i):
        at = pl.ds(pl.multiple_of(i * 256, 256), 256)
        acc[at, :] = jnp.dot(yt[at, :], zz[...], preferred_element_type=F32)


def early(bufs, left, right):
    n = len(bufs)
    return pl.pallas_call(
        functools.partial(early_kernel, n),
        out_shape=pltpu.VMEM((BLOCK, BLOCK), F32),
        in_specs=[ANY] * n + [VM] * 2,
        out_specs=VM,
        scratch_shapes=[
            pltpu.VMEM((BLOCK, n * TOK), BF16),
            pltpu.VMEM((n * TOK, BLOCK), BF16),
            pltpu.VMEM((n, TOK, 2 * BLOCK), BF16),
            pltpu.SemaphoreType.DMA((n,)),
        ],
        compiler_params=pltpu.CompilerParams(vmem_limit_bytes=20 << 20),
        cost_estimate=pl.CostEstimate(flops=6 * n * TOK * BLOCK * BLOCK, bytes_accessed=4 << 20, transcendentals=0),
        name="early",
    )(*[hbm(a) for a in bufs], vmem(left), vmem(right))


def final_kernel(n, *refs):
    bufs = refs[:n]
    acc, left, right, first, second, update, first_next, second_next = refs[n : n + 8]
    yt, zz, direction, m_out, v_out, u_out, sems = refs[n + 8 :]
    rotate(bufs, left, right, yt, zz)
    rows = 64

    def moment_copies(i):
        at = pl.ds(pl.multiple_of(i * rows, rows), rows)
        return (
            pltpu.make_async_copy(m_out.at[at, :], first_next.at[at, :], sems.at[i]),
            pltpu.make_async_copy(v_out.at[at, :], second_next.at[at, :], sems.at[16 + i]),
        )

    @pl.loop(0, BLOCK // rows)
    def _(i):
        at = pl.ds(pl.multiple_of(i * rows, rows), rows)
        rotated = acc[at, :] + jnp.dot(yt[at, :], zz[...], preferred_element_type=F32)
        m = 0.95 * first[at, :].astype(F32) + 0.05 * rotated
        v = 0.95 * second[at, :].astype(F32) + 0.05 * rotated * rotated
        m_out[at, :] = m.astype(BF16)
        v_out[at, :] = v.astype(BF16)
        scaled = v * (1.0 / CORRECT)
        root = scaled * lax.rsqrt(scaled) + 1e-08
        direction[at, :] = (m * (1.0 / CORRECT) * pl.reciprocal(root, approx=True)).astype(BF16)
        for copy in moment_copies(i):
            copy.start()

    def update_copy(i):
        at = pl.ds(pl.multiple_of(i * 256, 256), 256)
        return pltpu.make_async_copy(u_out.at[at, :], update.at[at, :], sems.at[32 + i])

    @pl.loop(0, 4)
    def _(i):
        at = pl.ds(pl.multiple_of(i * 256, 256), 256)
        back = jnp.dot(left[at, :], direction[...], preferred_element_type=F32).astype(BF16)
        u_out[at, :] = lax.dot_general(
            back, right[...], (((1,), (1,)), ((), ())), preferred_element_type=F32
        ).astype(BF16)
        update_copy(i).start()

    @pl.loop(0, BLOCK // rows)
    def _(i):
        for copy in moment_copies(i):
            copy.wait()

    @pl.loop(0, 4)
    def _(i):
        update_copy(i).wait()


def final(bufs, acc, left, right, first, second):
    n = len(bufs)
    square = jax.ShapeDtypeStruct((BLOCK, BLOCK), BF16)
    block = pltpu.VMEM((BLOCK, BLOCK), BF16)
    return pl.pallas_call(
        functools.partial(final_kernel, n),
        out_shape=[square] * 3,
        in_specs=[VM] * (n + 5),
        out_specs=[ANY] * 3,
        scratch_shapes=[
            pltpu.VMEM((BLOCK, n * TOK), BF16),
            pltpu.VMEM((n * TOK, BLOCK), BF16),
            block,
            block,
            block,
            block,
            pltpu.SemaphoreType.DMA((36,)),
        ],
        compiler_params=pltpu.CompilerParams(vmem_limit_bytes=20 << 20),
        cost_estimate=pl.CostEstimate(
            flops=(6 * n * TOK + 4 * BLOCK) * BLOCK * BLOCK, bytes_accessed=6 << 20, transcendentals=2 << 20
        ),
        name="final",
    )(*[vmem(a) for a in bufs], *[vmem(a) for a in (acc, left, right, first, second)])


def outer_kernel(core, mine, other, params, momentum, snap, local, due, params_next, momentum_next, local_next):
    own = (pl.program_id(0) // 4 == core[0]).astype(F32)
    total = own * mine[...].astype(F32) + (1.0 - own) * other[...].astype(F32)
    pseudo = total * (1.0 / 16)
    old, old_momentum = params[...], momentum[...]
    moment = 0.9 * old_momentum + pseudo
    stepped = old - 0.7 * (pseudo + 0.9 * moment)
    on = jnp.broadcast_to(due[:, :1], old.shape) == 1
    params_next[...] = jnp.where(on, stepped, old)
    momentum_next[...] = jnp.where(on, moment, old_momentum)
    kept = local[...].astype(F32)
    local_next[...] = jnp.where(on, stepped + (kept - snap[...].astype(F32)), kept).astype(BF16)


def outer(core, mine, other, params, momentum, snap, local, due):
    width = params.shape[1]
    whole = pl.BlockSpec((16, width), lambda i, c: (i, 0))
    part = pl.BlockSpec((16, width), lambda i, c: (i % 4, 0))
    return pl.pallas_call(
        outer_kernel,
        out_shape=[
            jax.ShapeDtypeStruct(params.shape, F32),
            jax.ShapeDtypeStruct(params.shape, F32),
            jax.ShapeDtypeStruct(params.shape, BF16),
        ],
        grid_spec=pltpu.PrefetchScalarGridSpec(
            num_scalar_prefetch=1,
            grid=(8,),
            in_specs=[part, part, whole, whole, whole, whole, pl.BlockSpec((16, 128), lambda i, c: (i, 0))],
            out_specs=[whole, whole, whole],
        ),
        compiler_params=pltpu.CompilerParams(vmem_limit_bytes=16 << 20),
        cost_estimate=pl.CostEstimate(flops=10 << 20, bytes_accessed=26 << 20, transcendentals=0),
        name="outer",
    )(core, mine, other, params, momentum, snap, local, due)


def after(array, others):
    return lax.optimization_barrier((array, *others))[0]


def added(one, two):
    return (one.astype(F32) + two.astype(F32)).astype(BF16)


def joined(mine, other, at):
    return lax.select(at == 0, jnp.concatenate([mine, other]), jnp.concatenate([other, mine]))


def per_device(
    tokens,
    out_grads,
    block_ids,
    left_basis,
    right_basis,
    first_moment,
    second_moment,
    outer_params,
    outer_momentum,
    snapshot,
    local_params,
    due_rows,
):
    replica = lax.axis_index("replica")
    y, core = replica // 4, replica % 2
    low, high = y % 2, y // 2
    at_a = jnp.where(core == 0, low ^ high, high)
    at_b = jnp.where(core == 0, high, low)

    def part(array, at):
        size = array.shape[0] // 2
        return lax.dynamic_slice_in_dim(array, at * size, size, 0)

    sends = pick(block_ids, tokens, out_grads)
    got = [to_owner(a, dx, dz) for a, (dx, dz) in zip(sends, SHIFTS)]
    left, right = left_basis[0, 0], right_basis[0, 0]

    def difference(half):
        at = half * 64
        params = lax.dynamic_slice_in_dim(outer_params, at, 64, 0)
        return (params - lax.dynamic_slice_in_dim(snapshot[0], at, 64, 0).astype(F32)).astype(BF16)

    def along_y(pair):
        quad = added(part(pair, at_a), to_y(part(pair, 1 - at_a), (1, 3)))
        return added(part(quad, at_b), to_y(part(quad, 1 - at_b), (3, 1)))

    def along_x(octet):
        total = added(octet, to_x(octet))
        return joined(total, to_y(total, (3, 1)), at_b)

    def nothing(rows):
        return lambda array: jnp.zeros((rows, array.shape[1]), BF16)

    always = replica >= 0
    pair = added(difference(core), to_core(difference(1 - core)))
    octet = lax.cond(always, along_y, nothing(16), after(pair, sends))
    rows = lax.cond(always, along_x, nothing(32), after(octet, got[:2]))
    rows = after(rows, got[2:4])
    rows = joined(rows, to_y(rows, (1, 3)), at_a)
    other = to_core(rows)
    due = jnp.broadcast_to(due_rows[:, None], (due_rows.shape[0], 128))
    outer_next, momentum_next, local_next = outer(
        core[None], rows, other, outer_params, outer_momentum, snapshot[0], local_params[0], due
    )

    acc = early([sends[-1]] + got[:EARLY], left, right)
    update, first_next, second_next = final(
        got[EARLY:], acc, left, right, first_moment[0, 0], second_moment[0, 0]
    )
    return (
        update[None, None],
        first_next[None, None],
        second_next[None, None],
        outer_next,
        momentum_next,
        local_next[None],
    )


def solution(mesh):
    return jax.shard_map(
        per_device,
        mesh=mesh,
        in_specs=(
            P(("replica", "fsdp"), None),
            P(("replica", "fsdp"), None),
            P(),
            P("replica", "fsdp", None, None),
            P("replica", "fsdp", None, None),
            P("replica", "fsdp", None, None),
            P("replica", "fsdp", None, None),
            P("fsdp", None),
            P("fsdp", None),
            P("replica", "fsdp", None),
            P("replica", "fsdp", None),
            P("fsdp"),
        ),
        out_specs=(
            P("replica", "fsdp", None, None),
            P("replica", "fsdp", None, None),
            P("replica", "fsdp", None, None),
            P("fsdp", None),
            P("fsdp", None),
            P("replica", "fsdp", None),
        ),
        check_vma=False,
    )
```

```python
import functools

import jax
import jax.numpy as jnp
from jax import lax
from jax.experimental import pallas as pl
from jax.experimental.pallas import tpu as pltpu
from jax.sharding import PartitionSpec as P

FW = 14336
BLOCK = 1024
TOK = 128
AXES = ("replica", "fsdp")
SHIFTS = ((1, 2), (1, 1), (1, 3), (0, 2), (0, 1), (0, 3), (1, 0))
FIRST = 4
CORRECT = 1.0 - 0.95**10
F32 = jnp.float32
BF16 = jnp.bfloat16
VM = pl.BlockSpec(memory_space=pltpu.VMEM)
ANY = pl.BlockSpec(memory_space=pl.ANY)


def place(index):
    replica, fsdp = divmod(index, 8)
    return replica // 4, replica // 2 % 2, replica % 2, fsdp // 4, fsdp % 4


def index_of(y, x_lo, core, x_hi, z):
    return ((y % 4 * 2 + x_lo % 2) * 2 + core % 2) * 8 + x_hi % 2 * 4 + z % 4


def moved(array, where):
    return lax.ppermute(array, AXES, [(s, index_of(*where(*place(s)))) for s in range(128)])


def to_owner(array, dx, dz):
    return moved(array, lambda y, x_lo, core, x_hi, z: (y, x_lo, core, x_hi + dx, z + dz))


def to_core(array):
    return moved(array, lambda y, x_lo, core, x_hi, z: (y, x_lo, core + 1, x_hi, z))


def to_x(array):
    return moved(array, lambda y, x_lo, core, x_hi, z: (y, x_lo + 1, core, x_hi, z))


def to_y(array, flips):
    return moved(array, lambda y, x_lo, core, x_hi, z: (y ^ flips[core], x_lo, core, x_hi, z))


def vmem(array):
    return pltpu.with_memory_space_constraint(array, pltpu.VMEM)


def hbm(array):
    return pltpu.with_memory_space_constraint(array, pltpu.HBM)


def pick_kernel(shifts, ids, tokens, out_grads, *rest):
    outs, (held, sems, out_sems) = rest[:-3], rest[-3:]
    columns = FW // BLOCK
    me = lax.axis_index("fsdp")
    x_hi, z = me // 4, me % 4
    copies = []
    for i, (dx, dz) in enumerate(shifts):
        owner = (x_hi + dx) % 2 * 4 + (z + dz) % 4
        block = ids[owner]
        row = pl.multiple_of(block // columns * BLOCK, BLOCK)
        col = pl.multiple_of(block % columns * BLOCK, BLOCK)
        for k, (source, at) in enumerate(((tokens, row), (out_grads, col))):
            copy = pltpu.make_async_copy(
                source.at[:, pl.ds(at, BLOCK)], held.at[i, :, pl.ds(k * BLOCK, BLOCK)], sems.at[2 * i + k]
            )
            copy.start()
            copies.append(copy)
    stores = []
    for i, out in enumerate(outs):
        copies[2 * i].wait()
        copies[2 * i + 1].wait()
        store = pltpu.make_async_copy(held.at[i], out, out_sems.at[i])
        store.start()
        stores.append(store)
    for store in stores:
        store.wait()


def pick(block_ids, tokens, out_grads, shifts):
    n = len(shifts)
    return pl.pallas_call(
        functools.partial(pick_kernel, shifts),
        out_shape=[pltpu.HBM((TOK, 2 * BLOCK), BF16)] * n,
        in_specs=[pl.BlockSpec(memory_space=pltpu.SMEM), ANY, ANY],
        out_specs=[ANY] * n,
        scratch_shapes=[
            pltpu.VMEM((n, TOK, 2 * BLOCK), BF16),
            pltpu.SemaphoreType.DMA((2 * n,)),
            pltpu.SemaphoreType.DMA((n,)),
        ],
        compiler_params=pltpu.CompilerParams(vmem_limit_bytes=6 << 20),
        cost_estimate=pl.CostEstimate(flops=0, bytes_accessed=8 << 20, transcendentals=0),
        name="pick",
    )(block_ids, hbm(tokens), hbm(out_grads))


def rotate(bufs, left, right, yt, zz):
    step = 256

    @pl.loop(0, BLOCK // step)
    def _(j):
        at = pl.ds(pl.multiple_of(j * step, step), step)
        xs = jnp.concatenate([b[:, :BLOCK] for b in bufs], axis=0)
        ds = jnp.concatenate([b[:, BLOCK:] for b in bufs], axis=0)
        yt[at, :] = jnp.dot(xs, left[:, at], preferred_element_type=F32).T.astype(BF16)
        zz[:, at] = jnp.dot(ds, right[:, at], preferred_element_type=F32).astype(BF16)


def early_kernel(n, more, *refs):
    sources, (left_in, right_in), refs = refs[:n], refs[n : n + 2], refs[n + 2 :]
    acc_in, refs = (refs[0], refs[1:]) if more else (None, refs)
    acc_out, yt, zz, held, left, right, acc, sems = refs
    copies = [pltpu.make_async_copy(source, held.at[i], sems.at[i]) for i, source in enumerate(sources)]
    copies.append(pltpu.make_async_copy(left_in, left, sems.at[n]))
    copies.append(pltpu.make_async_copy(right_in, right, sems.at[n + 1]))
    if more:
        copies.append(pltpu.make_async_copy(acc_in, acc, sems.at[n + 2]))
    for copy in copies:
        copy.start()
    for copy in copies[: n + 2]:
        copy.wait()
    rotate([held.at[i] for i in range(n)], left, right, yt, zz)
    if more:
        copies[-1].wait()

    def store(i):
        at = pl.ds(pl.multiple_of(i * 256, 256), 256)
        return pltpu.make_async_copy(acc.at[at, :], acc_out.at[at, :], sems.at[n + 3 + i])

    @pl.loop(0, 4)
    def _(i):
        at = pl.ds(pl.multiple_of(i * 256, 256), 256)
        term = jnp.dot(yt[at, :], zz[...], preferred_element_type=F32)
        acc[at, :] = acc[at, :] + term if more else term
        store(i).start()

    @pl.loop(0, 4)
    def _(i):
        store(i).wait()


def early(bufs, left, right, acc=()):
    n = len(bufs)
    block = pltpu.VMEM((BLOCK, BLOCK), BF16)
    return pl.pallas_call(
        functools.partial(early_kernel, n, len(acc)),
        out_shape=pltpu.HBM((BLOCK, BLOCK), F32),
        in_specs=[ANY] * (n + 2 + len(acc)),
        out_specs=ANY,
        scratch_shapes=[
            pltpu.VMEM((BLOCK, n * TOK), BF16),
            pltpu.VMEM((n * TOK, BLOCK), BF16),
            pltpu.VMEM((n, TOK, 2 * BLOCK), BF16),
            block,
            block,
            pltpu.VMEM((BLOCK, BLOCK), F32),
            pltpu.SemaphoreType.DMA((n + 7,)),
        ],
        compiler_params=pltpu.CompilerParams(vmem_limit_bytes=20 << 20),
        cost_estimate=pl.CostEstimate(flops=6 * n * TOK * BLOCK * BLOCK, bytes_accessed=4 << 20, transcendentals=0),
        name="early",
    )(*[hbm(a) for a in (*bufs, left, right, *acc)])


def final_kernel(n, *refs):
    operands, (update, first_next, second_next) = refs[: n + 5], refs[n + 5 : n + 8]
    held, yt, zz, direction, m_out, v_out, u_out, left, right, acc, first, second, sems, in_sems = refs[n + 8 :]
    places = [held.at[i] for i in range(n)] + [left, right, acc, first, second]
    loads = [pltpu.make_async_copy(a, b, in_sems.at[i]) for i, (a, b) in enumerate(zip(operands, places))]
    for load in loads:
        load.start()
    for load in loads[: n + 2]:
        load.wait()
    rotate(places[:n], left, right, yt, zz)
    for load in loads[n + 2 :]:
        load.wait()
    rows = 256

    def moment_copies(i):
        at = pl.ds(pl.multiple_of(i * rows, rows), rows)
        return (
            pltpu.make_async_copy(m_out.at[at, :], first_next.at[at, :], sems.at[i]),
            pltpu.make_async_copy(v_out.at[at, :], second_next.at[at, :], sems.at[4 + i]),
        )

    @pl.loop(0, BLOCK // rows)
    def _(i):
        at = pl.ds(pl.multiple_of(i * rows, rows), rows)
        rotated = acc[at, :] + jnp.dot(yt[at, :], zz[...], preferred_element_type=F32)
        share = 0.05 * rotated
        m = 0.95 * first[at, :].astype(F32) + share
        v = 0.95 * second[at, :].astype(F32) + share * rotated
        m_out[at, :] = m.astype(BF16)
        v_out[at, :] = v.astype(BF16)
        scaled = v * CORRECT
        root = scaled * lax.rsqrt(scaled) + CORRECT * 1e-08
        direction[at, :] = (m * pltpu.reciprocal(root, approx=True)).astype(BF16)
        for copy in moment_copies(i):
            copy.start()

    def update_copy(i):
        at = pl.ds(pl.multiple_of(i * 256, 256), 256)
        return pltpu.make_async_copy(u_out.at[at, :], update.at[at, :], sems.at[8 + i])

    @pl.loop(0, 4)
    def _(i):
        at = pl.ds(pl.multiple_of(i * 256, 256), 256)
        back = jnp.dot(left[at, :], direction[...], preferred_element_type=F32).astype(BF16)
        u_out[at, :] = lax.dot_general(
            back, right[...], (((1,), (1,)), ((), ())), preferred_element_type=F32
        ).astype(BF16)
        update_copy(i).start()

    @pl.loop(0, BLOCK // rows)
    def _(i):
        for copy in moment_copies(i):
            copy.wait()

    @pl.loop(0, 4)
    def _(i):
        update_copy(i).wait()


def final(bufs, acc, left, right, first, second):
    n = len(bufs)
    square = jax.ShapeDtypeStruct((BLOCK, BLOCK), BF16)
    block = pltpu.VMEM((BLOCK, BLOCK), BF16)
    return pl.pallas_call(
        functools.partial(final_kernel, n),
        out_shape=[square] * 3,
        in_specs=[ANY] * (n + 5),
        out_specs=[ANY] * 3,
        scratch_shapes=[
            pltpu.VMEM((n, TOK, 2 * BLOCK), BF16),
            pltpu.VMEM((BLOCK, n * TOK), BF16),
            pltpu.VMEM((n * TOK, BLOCK), BF16),
            *[block] * 6,
            pltpu.VMEM((BLOCK, BLOCK), F32),
            *[block] * 2,
            pltpu.SemaphoreType.DMA((12,)),
            pltpu.SemaphoreType.DMA((n + 5,)),
        ],
        compiler_params=pltpu.CompilerParams(vmem_limit_bytes=28 << 20),
        cost_estimate=pl.CostEstimate(
            flops=(6 * n * TOK + 4 * BLOCK) * BLOCK * BLOCK, bytes_accessed=6 << 20, transcendentals=2 << 20
        ),
        name="final",
    )(*[hbm(a) for a in (*bufs, left, right, acc, first, second)])


def outer_kernel(half, total, params, momentum, snap, local, due, *rest):
    params_next, momentum_next, local_next = rest[-3:]
    pseudo = total[...].astype(F32) * (1.0 / 16)
    old, old_momentum = params[...], momentum[...]
    moment = 0.9 * old_momentum + pseudo
    stepped = old - 0.7 * (pseudo + 0.9 * moment)
    on = jnp.broadcast_to(due[:, :1], old.shape) == 1
    params_next[...] = jnp.where(on, stepped, old)
    momentum_next[...] = jnp.where(on, moment, old_momentum)
    kept = local[...].astype(F32)
    local_next[...] = jnp.where(on, stepped + (kept - snap[...].astype(F32)), kept).astype(BF16)


def outer(half, total, params, momentum, snap, local, due, into=()):
    width = params.shape[1]
    whole = pl.BlockSpec((16, width), lambda i, h: (h[0] * 4 + i, 0))
    part = pl.BlockSpec((16, width), lambda i, h: (i, 0))
    return pl.pallas_call(
        outer_kernel,
        out_shape=[
            pltpu.HBM(params.shape, F32),
            pltpu.HBM(params.shape, F32),
            pltpu.HBM(params.shape, BF16),
        ],
        grid_spec=pltpu.PrefetchScalarGridSpec(
            num_scalar_prefetch=1,
            grid=(4,),
            in_specs=[part, whole, whole, whole, whole, pl.BlockSpec((16, 128), lambda i, h: (h[0] * 4 + i, 0))]
            + [ANY] * len(into),
            out_specs=[whole, whole, whole],
        ),
        input_output_aliases={7 + i: i for i in range(len(into))},
        compiler_params=pltpu.CompilerParams(vmem_limit_bytes=16 << 20),
        cost_estimate=pl.CostEstimate(flops=5 << 20, bytes_accessed=12 << 20, transcendentals=0),
        name="outer",
    )(half[None], total, params, momentum, snap, local, due, *into)


def after(array, others):
    return lax.optimization_barrier((array, *others))[0]


def added(one, two):
    return (one.astype(F32) + two.astype(F32)).astype(BF16)


def joined(mine, other, at):
    return lax.select(at == 0, jnp.concatenate([mine, other]), jnp.concatenate([other, mine]))


def per_device(
    tokens,
    out_grads,
    block_ids,
    left_basis,
    right_basis,
    first_moment,
    second_moment,
    outer_params,
    outer_momentum,
    snapshot,
    local_params,
    due_rows,
):
    replica = lax.axis_index("replica")
    y, core = replica // 4, replica % 2
    low, high = y % 2, y // 2
    at_a = jnp.where(core == 0, low ^ high, high)
    at_b = jnp.where(core == 0, high, low)

    def part(array, at):
        size = array.shape[0] // 2
        return lax.dynamic_slice_in_dim(array, at * size, size, 0)

    def difference(half):
        at = half * 64
        params = lax.dynamic_slice_in_dim(outer_params, at, 64, 0)
        return (params - lax.dynamic_slice_in_dim(snapshot[0], at, 64, 0).astype(F32)).astype(BF16)

    def along_y(pair, ids):
        quad = added(part(pair, at_a), to_y(part(pair, 1 - at_a), (1, 3)))
        rest = pick(ids, tokens, out_grads, (*SHIFTS[FIRST:], (0, 0)))
        return added(part(quad, at_b), to_y(part(quad, 1 - at_b), (3, 1))), *rest

    def no_along_y(pair, ids):
        return (pair[:16], *[pair[:32].reshape(-1, 2 * BLOCK)] * (len(SHIFTS) - FIRST + 1))

    def along_x(octet, sources):
        return added(octet, to_x(octet)), early(sources, left, right)

    def no_along_x(octet, sources):
        return octet, jnp.zeros((BLOCK, BLOCK), F32)

    def back(total, sources, acc):
        return joined(total, to_y(total, (3, 1)), at_b), early(sources, left, right, [acc])

    def no_back(total, sources, acc):
        return jnp.concatenate([total, total]), jnp.zeros((BLOCK, BLOCK), F32)

    always = replica >= 0
    left, right = left_basis[0, 0], right_basis[0, 0]
    pair = added(difference(core), to_core(difference(1 - core)))
    sends = pick(block_ids, tokens, out_grads, SHIFTS[:FIRST])
    got = [to_owner(a, dx, dz) for a, (dx, dz) in zip(sends, SHIFTS)]
    octet, *rest = lax.cond(always, along_y, no_along_y, after(pair, sends), block_ids)
    got += [to_owner(a, dx, dz) for a, (dx, dz) in zip(rest, SHIFTS[FIRST:])]
    total, acc = lax.cond(always, along_x, no_along_x, after(octet, got[:2]), [rest[-1], *got[:2]])
    rows, acc = lax.cond(always, back, no_back, after(total, got[2:FIRST]), got[2:FIRST], acc)
    rows = after(rows, got[FIRST:])
    rows = joined(rows, to_y(rows, (1, 3)), at_a)
    update, first_next, second_next = final(got[FIRST:], acc, left, right, first_moment[0, 0], second_moment[0, 0])
    rows = after(rows, [update])
    other = to_core(rows)
    due = jnp.broadcast_to(due_rows[:, None], (due_rows.shape[0], 128))
    state = (outer_params, outer_momentum, snapshot[0], local_params[0], due)
    halves = outer(core, rows, *state)
    outer_next, momentum_next, local_next = outer(1 - core, other, *state, into=halves)
    return (
        update[None, None],
        first_next[None, None],
        second_next[None, None],
        outer_next,
        momentum_next,
        local_next[None],
    )


def solution(mesh):
    return jax.shard_map(
        per_device,
        mesh=mesh,
        in_specs=(
            P(("replica", "fsdp"), None),
            P(("replica", "fsdp"), None),
            P(),
            P("replica", "fsdp", None, None),
            P("replica", "fsdp", None, None),
            P("replica", "fsdp", None, None),
            P("replica", "fsdp", None, None),
            P("fsdp", None),
            P("fsdp", None),
            P("replica", "fsdp", None),
            P("replica", "fsdp", None),
            P("fsdp"),
        ),
        out_specs=(
            P("replica", "fsdp", None, None),
            P("replica", "fsdp", None, None),
            P("replica", "fsdp", None, None),
            P("fsdp", None),
            P("fsdp", None),
            P("replica", "fsdp", None),
        ),
        check_vma=False,
    )
```

```python
import functools

import jax
import jax.numpy as jnp
from jax import lax
from jax.experimental import pallas as pl
from jax.experimental.pallas import tpu as pltpu
from jax.sharding import PartitionSpec as P

FW = 14336
BLOCK = 1024
TOK = 128
AXES = ("replica", "fsdp")
SHIFTS = ((1, 2), (1, 1), (1, 3), (0, 2), (0, 1), (0, 3), (1, 0))
FIRST = 4
EARLY = 4
CORRECT = 1.0 - 0.95**10
F32 = jnp.float32
BF16 = jnp.bfloat16
VM = pl.BlockSpec(memory_space=pltpu.VMEM)
ANY = pl.BlockSpec(memory_space=pl.ANY)


def place(index):
    replica, fsdp = divmod(index, 8)
    return replica // 4, replica // 2 % 2, replica % 2, fsdp // 4, fsdp % 4


def index_of(y, x_lo, core, x_hi, z):
    return ((y % 4 * 2 + x_lo % 2) * 2 + core % 2) * 8 + x_hi % 2 * 4 + z % 4


def moved(array, where):
    return lax.ppermute(array, AXES, [(s, index_of(*where(*place(s)))) for s in range(128)])


def to_owner(array, dx, dz):
    return moved(array, lambda y, x_lo, core, x_hi, z: (y, x_lo, core, x_hi + dx, z + dz))


def to_core(array):
    return moved(array, lambda y, x_lo, core, x_hi, z: (y, x_lo, core + 1, x_hi, z))


def to_x(array):
    return moved(array, lambda y, x_lo, core, x_hi, z: (y, x_lo + 1, core, x_hi, z))


def to_y(array, flips):
    return moved(array, lambda y, x_lo, core, x_hi, z: (y ^ flips[core], x_lo, core, x_hi, z))


def vmem(array):
    return pltpu.with_memory_space_constraint(array, pltpu.VMEM)


def hbm(array):
    return pltpu.with_memory_space_constraint(array, pltpu.HBM)


def pick_kernel(shifts, ids, tokens, out_grads, *rest):
    outs, (held, sems, out_sems) = rest[:-3], rest[-3:]
    columns = FW // BLOCK
    me = lax.axis_index("fsdp")
    x_hi, z = me // 4, me % 4
    copies = []
    for i, (dx, dz) in enumerate(shifts):
        owner = (x_hi + dx) % 2 * 4 + (z + dz) % 4
        block = ids[owner]
        row = pl.multiple_of(block // columns * BLOCK, BLOCK)
        col = pl.multiple_of(block % columns * BLOCK, BLOCK)
        for k, (source, at) in enumerate(((tokens, row), (out_grads, col))):
            copy = pltpu.make_async_copy(
                source.at[:, pl.ds(at, BLOCK)], held.at[i, :, pl.ds(k * BLOCK, BLOCK)], sems.at[2 * i + k]
            )
            copy.start()
            copies.append(copy)
    stores = []
    for i, out in enumerate(outs):
        copies[2 * i].wait()
        copies[2 * i + 1].wait()
        store = pltpu.make_async_copy(held.at[i], out, out_sems.at[i])
        store.start()
        stores.append(store)
    for store in stores:
        store.wait()


def pick(block_ids, tokens, out_grads, shifts):
    n = len(shifts)
    return pl.pallas_call(
        functools.partial(pick_kernel, shifts),
        out_shape=[pltpu.HBM((TOK, 2 * BLOCK), BF16)] * n,
        in_specs=[pl.BlockSpec(memory_space=pltpu.SMEM), ANY, ANY],
        out_specs=[ANY] * n,
        scratch_shapes=[
            pltpu.VMEM((n, TOK, 2 * BLOCK), BF16),
            pltpu.SemaphoreType.DMA((2 * n,)),
            pltpu.SemaphoreType.DMA((n,)),
        ],
        compiler_params=pltpu.CompilerParams(vmem_limit_bytes=6 << 20),
        cost_estimate=pl.CostEstimate(flops=0, bytes_accessed=8 << 20, transcendentals=0),
        name="pick",
    )(block_ids, hbm(tokens), hbm(out_grads))


def rotate(bufs, left, right, yt, zz):
    step = 256

    @pl.loop(0, BLOCK // step)
    def _(j):
        at = pl.ds(pl.multiple_of(j * step, step), step)
        xs = jnp.concatenate([b[:, :BLOCK] for b in bufs], axis=0)
        ds = jnp.concatenate([b[:, BLOCK:] for b in bufs], axis=0)
        yt[at, :] = jnp.dot(xs, left[:, at], preferred_element_type=F32).T.astype(BF16)
        zz[:, at] = jnp.dot(ds, right[:, at], preferred_element_type=F32).astype(BF16)


def early_kernel(n, more, *refs):
    sources, (left_in, right_in), refs = refs[:n], refs[n : n + 2], refs[n + 2 :]
    acc_in, refs = (refs[0], refs[1:]) if more else (None, refs)
    acc_out, yt, zz, held, left, right, acc, sems = refs
    copies = [pltpu.make_async_copy(source, held.at[i], sems.at[i]) for i, source in enumerate(sources)]
    copies.append(pltpu.make_async_copy(left_in, left, sems.at[n]))
    copies.append(pltpu.make_async_copy(right_in, right, sems.at[n + 1]))
    if more:
        copies.append(pltpu.make_async_copy(acc_in, acc, sems.at[n + 2]))
    for copy in copies[: n + 2]:
        copy.start()
    for copy in copies[: n + 2]:
        copy.wait()
    if more:
        copies[-1].start()
    rotate([held.at[i] for i in range(n)], left, right, yt, zz)
    if more:
        copies[-1].wait()

    def store(i):
        at = pl.ds(pl.multiple_of(i * 256, 256), 256)
        return pltpu.make_async_copy(acc.at[at, :], acc_out.at[at, :], sems.at[n + 3 + i])

    @pl.loop(0, 4)
    def _(i):
        at = pl.ds(pl.multiple_of(i * 256, 256), 256)
        term = jnp.dot(yt[at, :], zz[...], preferred_element_type=F32)
        acc[at, :] = acc[at, :] + term if more else term
        store(i).start()

    @pl.loop(0, 4)
    def _(i):
        store(i).wait()


def early(bufs, left, right, acc=()):
    n = len(bufs)
    block = pltpu.VMEM((BLOCK, BLOCK), BF16)
    return pl.pallas_call(
        functools.partial(early_kernel, n, len(acc)),
        out_shape=pltpu.HBM((BLOCK, BLOCK), F32),
        in_specs=[ANY] * (n + 2 + len(acc)),
        out_specs=ANY,
        scratch_shapes=[
            pltpu.VMEM((BLOCK, n * TOK), BF16),
            pltpu.VMEM((n * TOK, BLOCK), BF16),
            pltpu.VMEM((n, TOK, 2 * BLOCK), BF16),
            block,
            block,
            pltpu.VMEM((BLOCK, BLOCK), F32),
            pltpu.SemaphoreType.DMA((n + 7,)),
        ],
        compiler_params=pltpu.CompilerParams(vmem_limit_bytes=20 << 20),
        cost_estimate=pl.CostEstimate(flops=6 * n * TOK * BLOCK * BLOCK, bytes_accessed=4 << 20, transcendentals=0),
        name="early",
    )(*[hbm(a) for a in (*bufs, left, right, *acc)])


def hold_kernel(gate, *refs):
    sources, outs, sems = refs[:2], refs[2:4], refs[4]
    copies = [pltpu.make_async_copy(a, b, sems.at[i]) for i, (a, b) in enumerate(zip(sources, outs))]
    for copy in copies:
        copy.start()
    for copy in copies:
        copy.wait()


def hold(gate, arrays):
    return pl.pallas_call(
        hold_kernel,
        out_shape=[pltpu.VMEM(a.shape, a.dtype) for a in arrays],
        in_specs=[ANY] * 3,
        out_specs=[VM] * 2,
        scratch_shapes=[pltpu.SemaphoreType.DMA((2,))],
        compiler_params=pltpu.CompilerParams(vmem_limit_bytes=1 << 20),
        cost_estimate=pl.CostEstimate(flops=0, bytes_accessed=8 << 20, transcendentals=0),
        name="hold",
    )(*[hbm(a) for a in (gate, *arrays)])


def final_kernel(n, *refs):
    left, right, refs = refs[0], refs[1], refs[2:]
    operands, carried, refs = refs[: n + 3], refs[n + 3 : n + 7], refs[n + 7 :]
    (update, first_next, second_next), kept, refs = refs[:3], refs[3:7], refs[7:]
    held, yt, zz, direction, m_out, v_out, u_out, acc, first, second, sems, in_sems = refs
    places = [held.at[i] for i in range(n)] + [acc, first, second]
    pairs = [*zip(operands, places), *zip(carried, kept)]
    loads = [pltpu.make_async_copy(a, b, in_sems.at[i]) for i, (a, b) in enumerate(pairs)]
    for load in loads[:n]:
        load.start()
    for load in loads[:n]:
        load.wait()
    for load in loads[n:]:
        load.start()
    rotate(places[:n], left, right, yt, zz)
    for load in loads[n : n + 3]:
        load.wait()
    rows = 256

    def moment_copies(i):
        at = pl.ds(pl.multiple_of(i * rows, rows), rows)
        return (
            pltpu.make_async_copy(m_out.at[at, :], first_next.at[at, :], sems.at[i]),
            pltpu.make_async_copy(v_out.at[at, :], second_next.at[at, :], sems.at[4 + i]),
        )

    @pl.loop(0, BLOCK // rows, unroll=True)
    def _(i):
        at = pl.ds(pl.multiple_of(i * rows, rows), rows)
        rotated = acc[at, :] + jnp.dot(yt[at, :], zz[...], preferred_element_type=F32)
        share = 0.05 * rotated
        m = 0.95 * first[at, :].astype(F32) + share
        v = 0.95 * second[at, :].astype(F32) + share * rotated
        m_out[at, :] = m.astype(BF16)
        v_out[at, :] = v.astype(BF16)
        scaled = v * CORRECT
        root = scaled * lax.rsqrt(scaled) + CORRECT * 1e-08
        direction[at, :] = (m * pltpu.reciprocal(root, approx=True)).astype(BF16)
        for copy in moment_copies(i):
            copy.start()

    def update_copy(i):
        at = pl.ds(pl.multiple_of(i * 256, 256), 256)
        return pltpu.make_async_copy(u_out.at[at, :], update.at[at, :], sems.at[8 + i])

    @pl.loop(0, 4)
    def _(i):
        at = pl.ds(pl.multiple_of(i * 256, 256), 256)
        back = jnp.dot(left[at, :], direction[...], preferred_element_type=F32).astype(BF16)
        u_out[at, :] = lax.dot_general(
            back, right[...], (((1,), (1,)), ((), ())), preferred_element_type=F32
        ).astype(BF16)
        update_copy(i).start()

    @pl.loop(0, BLOCK // rows)
    def _(i):
        for copy in moment_copies(i):
            copy.wait()

    @pl.loop(0, 4)
    def _(i):
        update_copy(i).wait()

    for load in loads[n + 3 :]:
        load.wait()


def final(bufs, acc, left, right, first, second, carried):
    n = len(bufs)
    square = jax.ShapeDtypeStruct((BLOCK, BLOCK), BF16)
    block = pltpu.VMEM((BLOCK, BLOCK), BF16)
    return pl.pallas_call(
        functools.partial(final_kernel, n),
        out_shape=[square] * 3 + [pltpu.VMEM(a.shape, a.dtype) for a in carried],
        in_specs=[VM] * 2 + [ANY] * (n + 7),
        out_specs=[ANY] * 3 + [VM] * 4,
        scratch_shapes=[
            pltpu.VMEM((n, TOK, 2 * BLOCK), BF16),
            pltpu.VMEM((BLOCK, n * TOK), BF16),
            pltpu.VMEM((n * TOK, BLOCK), BF16),
            *[block] * 4,
            pltpu.VMEM((BLOCK, BLOCK), F32),
            *[block] * 2,
            pltpu.SemaphoreType.DMA((12,)),
            pltpu.SemaphoreType.DMA((n + 7,)),
        ],
        compiler_params=pltpu.CompilerParams(vmem_limit_bytes=28 << 20),
        cost_estimate=pl.CostEstimate(
            flops=(6 * n * TOK + 4 * BLOCK) * BLOCK * BLOCK, bytes_accessed=6 << 20, transcendentals=2 << 20
        ),
        name="final",
    )(vmem(left), vmem(right), *[hbm(a) for a in (*bufs, acc, first, second, *carried)])


def outer_kernel(half, total, params, momentum, snap, local, due, *rest):
    nexts, (params_out, momentum_out, local_out, sems) = rest[-7:-4], rest[-4:]

    def stores(i):
        at = pl.ds(pl.multiple_of((half[0] * 4 + i) * 16, 16), 16)
        mine = pl.ds(pl.multiple_of(i * 16, 16), 16)
        return [
            pltpu.make_async_copy(out.at[mine, :], to.at[at, :], sems.at[3 * i + k])
            for k, (out, to) in enumerate(zip((params_out, momentum_out, local_out), nexts))
        ]

    @pl.loop(0, 4)
    def _(i):
        at = pl.ds(pl.multiple_of((half[0] * 4 + i) * 16, 16), 16)
        mine = pl.ds(pl.multiple_of(i * 16, 16), 16)
        pseudo = total[mine, :].astype(F32) * (1.0 / 16)
        old, old_momentum = params[at, :], momentum[at, :]
        moment = 0.9 * old_momentum + pseudo
        stepped = old - 0.7 * (pseudo + 0.9 * moment)
        on = jnp.concatenate([due[at, :]] * (old.shape[1] // 128), axis=1) == 1
        params_out[mine, :] = jnp.where(on, stepped, old)
        momentum_out[mine, :] = jnp.where(on, moment, old_momentum)
        kept = local[at, :].astype(F32)
        local_out[mine, :] = jnp.where(on, stepped + (kept - snap[at, :].astype(F32)), kept).astype(BF16)
        for store in stores(i):
            store.start()

    @pl.loop(0, 4)
    def _(i):
        for store in stores(i):
            store.wait()


def outer(half, total, params, momentum, snap, local, due, into=()):
    rows, width = total.shape
    return pl.pallas_call(
        outer_kernel,
        out_shape=[
            pltpu.HBM(params.shape, F32),
            pltpu.HBM(params.shape, F32),
            pltpu.HBM(params.shape, BF16),
        ],
        in_specs=[pl.BlockSpec(memory_space=pltpu.SMEM)] + [VM] * 6 + [ANY] * len(into),
        out_specs=[ANY] * 3,
        scratch_shapes=[
            pltpu.VMEM((rows, width), F32),
            pltpu.VMEM((rows, width), F32),
            pltpu.VMEM((rows, width), BF16),
            pltpu.SemaphoreType.DMA((12,)),
        ],
        input_output_aliases={7 + i: i for i in range(len(into))},
        compiler_params=pltpu.CompilerParams(vmem_limit_bytes=16 << 20),
        cost_estimate=pl.CostEstimate(flops=5 << 20, bytes_accessed=12 << 20, transcendentals=0),
        name="outer",
    )(half[None], *[vmem(a) for a in (total, params, momentum, snap, local, due)], *into)


def after(array, others):
    return lax.optimization_barrier((array, *others))[0]


def added(one, two):
    return (one.astype(F32) + two.astype(F32)).astype(BF16)


def joined(mine, other, at):
    return lax.select(at == 0, jnp.concatenate([mine, other]), jnp.concatenate([other, mine]))


def per_device(
    tokens,
    out_grads,
    block_ids,
    left_basis,
    right_basis,
    first_moment,
    second_moment,
    outer_params,
    outer_momentum,
    snapshot,
    local_params,
    due_rows,
):
    replica = lax.axis_index("replica")
    y, core = replica // 4, replica % 2
    low, high = y % 2, y // 2
    at_a = jnp.where(core == 0, low ^ high, high)
    at_b = jnp.where(core == 0, high, low)

    def part(array, at):
        size = array.shape[0] // 2
        return lax.dynamic_slice_in_dim(array, at * size, size, 0)

    def difference(half):
        at = half * 64
        params = lax.dynamic_slice_in_dim(outer_params, at, 64, 0)
        return (params - lax.dynamic_slice_in_dim(snapshot[0], at, 64, 0).astype(F32)).astype(BF16)

    def along_y(pair, ids):
        quad = added(part(pair, at_a), to_y(part(pair, 1 - at_a), (1, 3)))
        rest = pick(ids, tokens, out_grads, (*SHIFTS[FIRST:], (0, 0)))
        return added(part(quad, at_b), to_y(part(quad, 1 - at_b), (3, 1))), *rest

    def no_along_y(pair, ids):
        return (pair[:16], *[pair[:32].reshape(-1, 2 * BLOCK)] * (len(SHIFTS) - FIRST + 1))

    def along_x(octet, sources):
        return added(octet, to_x(octet)), early(sources, left, right)

    def no_along_x(octet, sources):
        return octet, jnp.zeros((BLOCK, BLOCK), F32)

    def back(total, sources, acc):
        return joined(total, to_y(total, (3, 1)), at_b), early(sources, left, right, [acc])

    def no_back(total, sources, acc):
        return jnp.concatenate([total, total]), jnp.zeros((BLOCK, BLOCK), F32)

    always = replica >= 0
    left, right = left_basis[0, 0], right_basis[0, 0]
    pair = added(difference(core), to_core(difference(1 - core)))
    sends = pick(block_ids, tokens, out_grads, SHIFTS[:FIRST])
    got = [to_owner(a, dx, dz) for a, (dx, dz) in zip(sends, SHIFTS)]
    octet, *rest = lax.cond(always, along_y, no_along_y, after(pair, sends), block_ids)
    got += [to_owner(a, dx, dz) for a, (dx, dz) in zip(rest, SHIFTS[FIRST:])]
    total, acc = lax.cond(always, along_x, no_along_x, after(octet, got[:2]), [rest[-1], *got[:2]])
    rows, acc = lax.cond(always, back, no_back, after(total, got[2:EARLY]), got[2:EARLY], acc)
    left, right = hold(acc, (left, right))
    rows = after(rows, [*got[EARLY:], left])
    rows = joined(rows, to_y(rows, (1, 3)), at_a)
    carried = (outer_params, outer_momentum, snapshot[0], local_params[0])
    update, first_next, second_next, *carried = final(
        got[EARLY:], acc, left, right, first_moment[0, 0], second_moment[0, 0], carried
    )
    rows = after(rows, [update])
    other = to_core(rows)
    due = jnp.broadcast_to(due_rows[:, None], (due_rows.shape[0], 128))
    state = (*carried, due)
    halves = outer(core, rows, *state)
    outer_next, momentum_next, local_next = outer(1 - core, other, *state, into=halves)
    return (
        update[None, None],
        first_next[None, None],
        second_next[None, None],
        outer_next,
        momentum_next,
        local_next[None],
    )


def solution(mesh):
    return jax.shard_map(
        per_device,
        mesh=mesh,
        in_specs=(
            P(("replica", "fsdp"), None),
            P(("replica", "fsdp"), None),
            P(),
            P("replica", "fsdp", None, None),
            P("replica", "fsdp", None, None),
            P("replica", "fsdp", None, None),
            P("replica", "fsdp", None, None),
            P("fsdp", None),
            P("fsdp", None),
            P("replica", "fsdp", None),
            P("replica", "fsdp", None),
            P("fsdp"),
        ),
        out_specs=(
            P("replica", "fsdp", None, None),
            P("replica", "fsdp", None, None),
            P("replica", "fsdp", None, None),
            P("fsdp", None),
            P("fsdp", None),
            P("replica", "fsdp", None),
        ),
        check_vma=False,
    )
```

```python
import functools

import jax
import jax.numpy as jnp
from jax import lax
from jax.experimental import pallas as pl
from jax.experimental.pallas import tpu as pltpu
from jax.sharding import PartitionSpec as P

FW = 14336
BLOCK = 1024
TOK = 128
AXES = ("replica", "fsdp")
SHIFTS = ((1, 2), (1, 1), (1, 3), (0, 2), (0, 1), (0, 3), (1, 0))
FIRST = 4
EARLY = 4
CORRECT = 1.0 - 0.95**10
F32 = jnp.float32
BF16 = jnp.bfloat16
VM = pl.BlockSpec(memory_space=pltpu.VMEM)
ANY = pl.BlockSpec(memory_space=pl.ANY)


def place(index):
    replica, fsdp = divmod(index, 8)
    return replica // 4, replica // 2 % 2, replica % 2, fsdp // 4, fsdp % 4


def index_of(y, x_lo, core, x_hi, z):
    return ((y % 4 * 2 + x_lo % 2) * 2 + core % 2) * 8 + x_hi % 2 * 4 + z % 4


def moved(array, where):
    return lax.ppermute(array, AXES, [(s, index_of(*where(*place(s)))) for s in range(128)])


def to_owner(array, dx, dz):
    return moved(array, lambda y, x_lo, core, x_hi, z: (y, x_lo, core, x_hi + dx, z + dz))


def to_core(array):
    return moved(array, lambda y, x_lo, core, x_hi, z: (y, x_lo, core + 1, x_hi, z))


def to_x(array):
    return moved(array, lambda y, x_lo, core, x_hi, z: (y, x_lo + 1, core, x_hi, z))


def to_y(array, flips):
    return moved(array, lambda y, x_lo, core, x_hi, z: (y ^ flips[core], x_lo, core, x_hi, z))


def vmem(array):
    return pltpu.with_memory_space_constraint(array, pltpu.VMEM)


def hbm(array):
    return pltpu.with_memory_space_constraint(array, pltpu.HBM)


def pick_kernel(shifts, ids, tokens, out_grads, *rest):
    outs, (held, sems, out_sems) = rest[:-3], rest[-3:]
    columns = FW // BLOCK
    me = lax.axis_index("fsdp")
    x_hi, z = me // 4, me % 4
    copies = []
    for i, (dx, dz) in enumerate(shifts):
        owner = (x_hi + dx) % 2 * 4 + (z + dz) % 4
        block = ids[owner]
        row = pl.multiple_of(block // columns * BLOCK, BLOCK)
        col = pl.multiple_of(block % columns * BLOCK, BLOCK)
        for k, (source, at) in enumerate(((tokens, row), (out_grads, col))):
            copy = pltpu.make_async_copy(
                source.at[:, pl.ds(at, BLOCK)], held.at[i, :, pl.ds(k * BLOCK, BLOCK)], sems.at[2 * i + k]
            )
            copy.start()
            copies.append(copy)
    stores = []
    for i, out in enumerate(outs):
        copies[2 * i].wait()
        copies[2 * i + 1].wait()
        store = pltpu.make_async_copy(held.at[i], out, out_sems.at[i])
        store.start()
        stores.append(store)
    for store in stores:
        store.wait()


def pick(block_ids, tokens, out_grads, shifts):
    n = len(shifts)
    return pl.pallas_call(
        functools.partial(pick_kernel, shifts),
        out_shape=[pltpu.HBM((TOK, 2 * BLOCK), BF16)] * n,
        in_specs=[pl.BlockSpec(memory_space=pltpu.SMEM), ANY, ANY],
        out_specs=[ANY] * n,
        scratch_shapes=[
            pltpu.VMEM((n, TOK, 2 * BLOCK), BF16),
            pltpu.SemaphoreType.DMA((2 * n,)),
            pltpu.SemaphoreType.DMA((n,)),
        ],
        compiler_params=pltpu.CompilerParams(vmem_limit_bytes=6 << 20),
        cost_estimate=pl.CostEstimate(flops=0, bytes_accessed=8 << 20, transcendentals=0),
        name="pick",
    )(block_ids, hbm(tokens), hbm(out_grads))


def rotate(bufs, left, right, yt, zz):
    xs = jnp.concatenate([b[:, :BLOCK] for b in bufs], axis=0)
    ds = jnp.concatenate([b[:, BLOCK:] for b in bufs], axis=0)
    for start in range(0, BLOCK, 512):
        at = slice(start, start + 512)
        yt[at, :] = jnp.dot(xs, left[:, at], preferred_element_type=F32).astype(BF16).T
        zz[:, at] = jnp.dot(ds, right[:, at], preferred_element_type=F32).astype(BF16)


def early_kernel(n, more, *refs):
    sources, (left_in, right_in), refs = refs[:n], refs[n : n + 2], refs[n + 2 :]
    acc_in, refs = (refs[0], refs[1:]) if more else (None, refs)
    acc_out, yt, zz, held, left, right, acc, sems = refs
    copies = [pltpu.make_async_copy(source, held.at[i], sems.at[i]) for i, source in enumerate(sources)]
    copies.append(pltpu.make_async_copy(left_in, left, sems.at[n]))
    copies.append(pltpu.make_async_copy(right_in, right, sems.at[n + 1]))
    if more:
        copies.append(pltpu.make_async_copy(acc_in, acc, sems.at[n + 2]))
    for copy in copies[: n + 2]:
        copy.start()
    for copy in copies[: n + 2]:
        copy.wait()
    if more:
        copies[-1].start()
    rotate([held.at[i] for i in range(n)], left, right, yt, zz)
    if more:
        copies[-1].wait()

    def store(i):
        at = pl.ds(pl.multiple_of(i * 256, 256), 256)
        return pltpu.make_async_copy(acc.at[at, :], acc_out.at[at, :], sems.at[n + 3 + i])

    @pl.loop(0, 4)
    def _(i):
        at = pl.ds(pl.multiple_of(i * 256, 256), 256)
        term = jnp.dot(yt[at, :], zz[...], preferred_element_type=F32)
        acc[at, :] = acc[at, :] + term if more else term
        store(i).start()

    @pl.loop(0, 4)
    def _(i):
        store(i).wait()


def early(bufs, left, right, acc=()):
    n = len(bufs)
    block = pltpu.VMEM((BLOCK, BLOCK), BF16)
    return pl.pallas_call(
        functools.partial(early_kernel, n, len(acc)),
        out_shape=pltpu.HBM((BLOCK, BLOCK), F32),
        in_specs=[ANY] * (n + 2 + len(acc)),
        out_specs=ANY,
        scratch_shapes=[
            pltpu.VMEM((BLOCK, n * TOK), BF16),
            pltpu.VMEM((n * TOK, BLOCK), BF16),
            pltpu.VMEM((n, TOK, 2 * BLOCK), BF16),
            block,
            block,
            pltpu.VMEM((BLOCK, BLOCK), F32),
            pltpu.SemaphoreType.DMA((n + 7,)),
        ],
        compiler_params=pltpu.CompilerParams(vmem_limit_bytes=20 << 20),
        cost_estimate=pl.CostEstimate(flops=6 * n * TOK * BLOCK * BLOCK, bytes_accessed=4 << 20, transcendentals=0),
        name="early",
    )(*[hbm(a) for a in (*bufs, left, right, *acc)])


def hold_kernel(gate, *refs):
    n = len(refs) // 2
    sources, outs, sems = refs[:n], refs[n : 2 * n], refs[2 * n]
    copies = [pltpu.make_async_copy(a, b, sems.at[i]) for i, (a, b) in enumerate(zip(sources, outs))]
    for copy in copies:
        copy.start()
    for copy in copies:
        copy.wait()


def hold(gate, arrays):
    return pl.pallas_call(
        hold_kernel,
        out_shape=[pltpu.VMEM(a.shape, a.dtype) for a in arrays],
        in_specs=[ANY] * (len(arrays) + 1),
        out_specs=[VM] * len(arrays),
        scratch_shapes=[pltpu.SemaphoreType.DMA((len(arrays),))],
        compiler_params=pltpu.CompilerParams(vmem_limit_bytes=1 << 20),
        cost_estimate=pl.CostEstimate(flops=0, bytes_accessed=8 << 20, transcendentals=0),
        name="hold",
    )(*[hbm(a) for a in (gate, *arrays)])


def final_kernel(n, *refs):
    (left, right, first, second), refs = refs[:4], refs[4:]
    operands, carried, refs = refs[: n + 1], refs[n + 1 : n + 5], refs[n + 5 :]
    (update, first_next, second_next), kept, refs = refs[:3], refs[3:7], refs[7:]
    held, yt, zz, direction, m_out, v_out, u_out, acc, sems, in_sems = refs
    places = [held.at[i] for i in range(n)] + [acc]
    pairs = [*zip(operands, places), *zip(carried, kept)]
    loads = [pltpu.make_async_copy(a, b, in_sems.at[i]) for i, (a, b) in enumerate(pairs)]
    for load in loads[: n + 1]:
        load.start()
    for load in loads[:n]:
        load.wait()
    rotate(places[:n], left, right, yt, zz)
    loads[n].wait()
    for load in loads[n + 1 :]:
        load.start()
    rows = 256

    def moment_copies(i):
        at = pl.ds(pl.multiple_of(i * rows, rows), rows)
        return (
            pltpu.make_async_copy(m_out.at[at, :], first_next.at[at, :], sems.at[i]),
            pltpu.make_async_copy(v_out.at[at, :], second_next.at[at, :], sems.at[4 + i]),
        )

    @pl.loop(0, BLOCK // rows, unroll=True)
    def _(i):
        at = pl.ds(pl.multiple_of(i * rows, rows), rows)
        rotated = acc[at, :] + jnp.dot(yt[at, :], zz[...], preferred_element_type=F32)
        share = 0.05 * rotated
        m = 0.95 * first[at, :].astype(F32) + share
        v = 0.95 * second[at, :].astype(F32) + share * rotated
        m_out[at, :] = m.astype(BF16)
        v_out[at, :] = v.astype(BF16)
        scaled = v * CORRECT
        root = scaled * lax.rsqrt(scaled) + CORRECT * 1e-08
        direction[at, :] = (m * pltpu.reciprocal(root, approx=True)).astype(BF16)
        for copy in moment_copies(i):
            copy.start()

    def update_copy(i):
        at = pl.ds(pl.multiple_of(i * 256, 256), 256)
        return pltpu.make_async_copy(u_out.at[at, :], update.at[at, :], sems.at[8 + i])

    @pl.loop(0, 4)
    def _(i):
        at = pl.ds(pl.multiple_of(i * 256, 256), 256)
        back = jnp.dot(left[at, :], direction[...], preferred_element_type=F32).astype(BF16)
        u_out[at, :] = lax.dot_general(
            back, right[...], (((1,), (1,)), ((), ())), preferred_element_type=F32
        ).astype(BF16)
        update_copy(i).start()

    @pl.loop(0, BLOCK // rows)
    def _(i):
        for copy in moment_copies(i):
            copy.wait()

    @pl.loop(0, 4)
    def _(i):
        update_copy(i).wait()

    for load in loads[n + 1 :]:
        load.wait()


def final(bufs, acc, left, right, first, second, carried):
    n = len(bufs)
    square = jax.ShapeDtypeStruct((BLOCK, BLOCK), BF16)
    block = pltpu.VMEM((BLOCK, BLOCK), BF16)
    return pl.pallas_call(
        functools.partial(final_kernel, n),
        out_shape=[square] * 3 + [pltpu.VMEM(a.shape, a.dtype) for a in carried],
        in_specs=[VM] * 4 + [ANY] * (n + 5),
        out_specs=[ANY] * 3 + [VM] * 4,
        scratch_shapes=[
            pltpu.VMEM((n, TOK, 2 * BLOCK), BF16),
            pltpu.VMEM((BLOCK, n * TOK), BF16),
            pltpu.VMEM((n * TOK, BLOCK), BF16),
            *[block] * 4,
            pltpu.VMEM((BLOCK, BLOCK), F32),
            pltpu.SemaphoreType.DMA((12,)),
            pltpu.SemaphoreType.DMA((n + 5,)),
        ],
        compiler_params=pltpu.CompilerParams(vmem_limit_bytes=28 << 20),
        cost_estimate=pl.CostEstimate(
            flops=(6 * n * TOK + 4 * BLOCK) * BLOCK * BLOCK, bytes_accessed=6 << 20, transcendentals=2 << 20
        ),
        name="final",
    )(
        *[vmem(a) for a in (left, right, first, second)],
        *[hbm(a) for a in (*bufs, acc, *carried)],
    )


def outer_kernel(half, total, params, momentum, snap, local, due, *rest):
    nexts, (params_out, momentum_out, local_out, sems) = rest[-7:-4], rest[-4:]

    def stores(i):
        at = pl.ds(pl.multiple_of((half[0] * 4 + i) * 16, 16), 16)
        mine = pl.ds(pl.multiple_of(i * 16, 16), 16)
        return [
            pltpu.make_async_copy(out.at[mine, :], to.at[at, :], sems.at[3 * i + k])
            for k, (out, to) in enumerate(zip((params_out, momentum_out, local_out), nexts))
        ]

    @pl.loop(0, 4)
    def _(i):
        at = pl.ds(pl.multiple_of((half[0] * 4 + i) * 16, 16), 16)
        mine = pl.ds(pl.multiple_of(i * 16, 16), 16)
        pseudo = total[mine, :].astype(F32) * (1.0 / 16)
        old, old_momentum = params[at, :], momentum[at, :]
        moment = 0.9 * old_momentum + pseudo
        stepped = old - 0.7 * (pseudo + 0.9 * moment)
        on = jnp.concatenate([due[at, :]] * (old.shape[1] // 128), axis=1) == 1
        params_out[mine, :] = jnp.where(on, stepped, old)
        momentum_out[mine, :] = jnp.where(on, moment, old_momentum)
        kept = local[at, :].astype(F32)
        local_out[mine, :] = jnp.where(on, stepped + (kept - snap[at, :].astype(F32)), kept).astype(BF16)
        for store in stores(i):
            store.start()

    @pl.loop(0, 4)
    def _(i):
        for store in stores(i):
            store.wait()


def outer(half, total, params, momentum, snap, local, due, into=()):
    rows, width = total.shape
    return pl.pallas_call(
        outer_kernel,
        out_shape=[
            pltpu.HBM(params.shape, F32),
            pltpu.HBM(params.shape, F32),
            pltpu.HBM(params.shape, BF16),
        ],
        in_specs=[pl.BlockSpec(memory_space=pltpu.SMEM)] + [VM] * 6 + [ANY] * len(into),
        out_specs=[ANY] * 3,
        scratch_shapes=[
            pltpu.VMEM((rows, width), F32),
            pltpu.VMEM((rows, width), F32),
            pltpu.VMEM((rows, width), BF16),
            pltpu.SemaphoreType.DMA((12,)),
        ],
        input_output_aliases={7 + i: i for i in range(len(into))},
        compiler_params=pltpu.CompilerParams(vmem_limit_bytes=16 << 20),
        cost_estimate=pl.CostEstimate(flops=5 << 20, bytes_accessed=12 << 20, transcendentals=0),
        name="outer",
    )(half[None], *[vmem(a) for a in (total, params, momentum, snap, local, due)], *into)


def after(array, others):
    return lax.optimization_barrier((array, *others))[0]


def added(one, two):
    return (one.astype(F32) + two.astype(F32)).astype(BF16)


def joined(mine, other, at):
    return lax.select(at == 0, jnp.concatenate([mine, other]), jnp.concatenate([other, mine]))


def per_device(
    tokens,
    out_grads,
    block_ids,
    left_basis,
    right_basis,
    first_moment,
    second_moment,
    outer_params,
    outer_momentum,
    snapshot,
    local_params,
    due_rows,
):
    replica = lax.axis_index("replica")
    y, core = replica // 4, replica % 2
    low, high = y % 2, y // 2
    at_a = jnp.where(core == 0, low ^ high, high)
    at_b = jnp.where(core == 0, high, low)

    def part(array, at):
        size = array.shape[0] // 2
        return lax.dynamic_slice_in_dim(array, at * size, size, 0)

    def difference(half):
        at = half * 64
        params = lax.dynamic_slice_in_dim(outer_params, at, 64, 0)
        return (params - lax.dynamic_slice_in_dim(snapshot[0], at, 64, 0).astype(F32)).astype(BF16)

    def along_y(pair, ids):
        quad = added(part(pair, at_a), to_y(part(pair, 1 - at_a), (1, 3)))
        rest = pick(ids, tokens, out_grads, (*SHIFTS[FIRST:], (0, 0)))
        return added(part(quad, at_b), to_y(part(quad, 1 - at_b), (3, 1))), *rest

    def no_along_y(pair, ids):
        return (pair[:16], *[pair[:32].reshape(-1, 2 * BLOCK)] * (len(SHIFTS) - FIRST + 1))

    def along_x(octet, sources):
        return added(octet, to_x(octet)), early(sources, left, right)

    def no_along_x(octet, sources):
        return octet, jnp.zeros((BLOCK, BLOCK), F32)

    def back(total, sources, acc):
        return joined(total, to_y(total, (3, 1)), at_b), early(sources, left, right, [acc])

    def no_back(total, sources, acc):
        return jnp.concatenate([total, total]), jnp.zeros((BLOCK, BLOCK), F32)

    always = replica >= 0
    left, right = left_basis[0, 0], right_basis[0, 0]
    pair = added(difference(core), to_core(difference(1 - core)))
    sends = pick(block_ids, tokens, out_grads, SHIFTS[:FIRST])
    got = [to_owner(a, dx, dz) for a, (dx, dz) in zip(sends, SHIFTS)]
    octet, *rest = lax.cond(always, along_y, no_along_y, after(pair, sends), block_ids)
    got += [to_owner(a, dx, dz) for a, (dx, dz) in zip(rest, SHIFTS[FIRST:])]
    total, acc = lax.cond(always, along_x, no_along_x, after(octet, got[:2]), [rest[-1], *got[:2]])
    rows, acc = lax.cond(always, back, no_back, after(total, got[2:EARLY]), got[2:EARLY], acc)
    left, right, first, second = hold(acc, (left, right, first_moment[0, 0], second_moment[0, 0]))
    rows = after(rows, [*got[EARLY:], left])
    rows = joined(rows, to_y(rows, (1, 3)), at_a)
    carried = (outer_params, outer_momentum, snapshot[0], local_params[0])
    update, first_next, second_next, *carried = final(
        got[EARLY:], acc, left, right, first, second, carried
    )
    rows = after(rows, [update])
    other = to_core(rows)
    due = jnp.broadcast_to(due_rows[:, None], (due_rows.shape[0], 128))
    state = (*carried, due)
    halves = outer(core, rows, *state)
    outer_next, momentum_next, local_next = outer(1 - core, other, *state, into=halves)
    return (
        update[None, None],
        first_next[None, None],
        second_next[None, None],
        outer_next,
        momentum_next,
        local_next[None],
    )


def solution(mesh):
    return jax.shard_map(
        per_device,
        mesh=mesh,
        in_specs=(
            P(("replica", "fsdp"), None),
            P(("replica", "fsdp"), None),
            P(),
            P("replica", "fsdp", None, None),
            P("replica", "fsdp", None, None),
            P("replica", "fsdp", None, None),
            P("replica", "fsdp", None, None),
            P("fsdp", None),
            P("fsdp", None),
            P("replica", "fsdp", None),
            P("replica", "fsdp", None),
            P("fsdp"),
        ),
        out_specs=(
            P("replica", "fsdp", None, None),
            P("replica", "fsdp", None, None),
            P("replica", "fsdp", None, None),
            P("fsdp", None),
            P("fsdp", None),
            P("replica", "fsdp", None),
        ),
        check_vma=False,
    )
```

```python
import functools

import jax
import jax.numpy as jnp
from jax import lax
from jax.experimental import pallas as pl
from jax.experimental.pallas import tpu as pltpu
from jax.sharding import PartitionSpec as P

FW = 14336
BLOCK = 1024
TOK = 128
AXES = ("replica", "fsdp")
SHIFTS = ((1, 2), (1, 1), (1, 3), (0, 2), (0, 1), (0, 3), (1, 0))
FIRST = 4
EARLY = 4
CORRECT = 1.0 - 0.95**10
F32 = jnp.float32
BF16 = jnp.bfloat16
VM = pl.BlockSpec(memory_space=pltpu.VMEM)
ANY = pl.BlockSpec(memory_space=pl.ANY)


def place(index):
    replica, fsdp = divmod(index, 8)
    return replica // 4, replica // 2 % 2, replica % 2, fsdp // 4, fsdp % 4


def index_of(y, x_lo, core, x_hi, z):
    return ((y % 4 * 2 + x_lo % 2) * 2 + core % 2) * 8 + x_hi % 2 * 4 + z % 4


def moved(array, where):
    return lax.ppermute(array, AXES, [(s, index_of(*where(*place(s)))) for s in range(128)])


def to_owner(array, dx, dz):
    return moved(array, lambda y, x_lo, core, x_hi, z: (y, x_lo, core, x_hi + dx, z + dz))


def to_core(array):
    return moved(array, lambda y, x_lo, core, x_hi, z: (y, x_lo, core + 1, x_hi, z))


def to_x(array):
    return moved(array, lambda y, x_lo, core, x_hi, z: (y, x_lo + 1, core, x_hi, z))


def to_y(array, flips):
    return moved(array, lambda y, x_lo, core, x_hi, z: (y ^ flips[core], x_lo, core, x_hi, z))


def vmem(array):
    return pltpu.with_memory_space_constraint(array, pltpu.VMEM)


def hbm(array):
    return pltpu.with_memory_space_constraint(array, pltpu.HBM)


def pick_kernel(shifts, ids, tokens, out_grads, *rest):
    outs, (held, sems, out_sems) = rest[:-3], rest[-3:]
    columns = FW // BLOCK
    me = lax.axis_index("fsdp")
    x_hi, z = me // 4, me % 4
    copies = []
    for i, (dx, dz) in enumerate(shifts):
        owner = (x_hi + dx) % 2 * 4 + (z + dz) % 4
        block = ids[owner]
        row = pl.multiple_of(block // columns * BLOCK, BLOCK)
        col = pl.multiple_of(block % columns * BLOCK, BLOCK)
        for k, (source, at) in enumerate(((tokens, row), (out_grads, col))):
            copy = pltpu.make_async_copy(
                source.at[:, pl.ds(at, BLOCK)], held.at[i, :, pl.ds(k * BLOCK, BLOCK)], sems.at[2 * i + k]
            )
            copy.start()
            copies.append(copy)
    stores = []
    for i, out in enumerate(outs):
        copies[2 * i].wait()
        copies[2 * i + 1].wait()
        store = pltpu.make_async_copy(held.at[i], out, out_sems.at[i])
        store.start()
        stores.append(store)
    for store in stores:
        store.wait()


def pick(block_ids, tokens, out_grads, shifts):
    n = len(shifts)
    return pl.pallas_call(
        functools.partial(pick_kernel, shifts),
        out_shape=[pltpu.HBM((TOK, 2 * BLOCK), BF16)] * n,
        in_specs=[pl.BlockSpec(memory_space=pltpu.SMEM), ANY, ANY],
        out_specs=[ANY] * n,
        scratch_shapes=[
            pltpu.VMEM((n, TOK, 2 * BLOCK), BF16),
            pltpu.SemaphoreType.DMA((2 * n,)),
            pltpu.SemaphoreType.DMA((n,)),
        ],
        compiler_params=pltpu.CompilerParams(vmem_limit_bytes=6 << 20),
        cost_estimate=pl.CostEstimate(flops=0, bytes_accessed=8 << 20, transcendentals=0),
        name="pick",
    )(block_ids, hbm(tokens), hbm(out_grads))


def rotate(bufs, left, right, yt, zz):
    xs = jnp.concatenate([b[:, :BLOCK] for b in bufs], axis=0)
    ds = jnp.concatenate([b[:, BLOCK:] for b in bufs], axis=0)
    for start in range(0, BLOCK, 512):
        at = slice(start, start + 512)
        yt[at, :] = jnp.dot(xs, left[:, at], preferred_element_type=F32).astype(BF16).T
        zz[:, at] = jnp.dot(ds, right[:, at], preferred_element_type=F32).astype(BF16)


def early_kernel(n, more, *refs):
    sources, (left_in, right_in), refs = refs[:n], refs[n : n + 2], refs[n + 2 :]
    acc_in, refs = (refs[0], refs[1:]) if more else (None, refs)
    acc_out, yt, zz, held, left, right, acc, sems = refs
    copies = [pltpu.make_async_copy(source, held.at[i], sems.at[i]) for i, source in enumerate(sources)]
    copies.append(pltpu.make_async_copy(left_in, left, sems.at[n]))
    copies.append(pltpu.make_async_copy(right_in, right, sems.at[n + 1]))
    if more:
        copies.append(pltpu.make_async_copy(acc_in, acc, sems.at[n + 2]))
    for copy in copies[: n + 2]:
        copy.start()
    for copy in copies[: n + 2]:
        copy.wait()
    if more:
        copies[-1].start()
    rotate([held.at[i] for i in range(n)], left, right, yt, zz)
    if more:
        copies[-1].wait()

    def store(i):
        at = pl.ds(pl.multiple_of(i * 256, 256), 256)
        return pltpu.make_async_copy(acc.at[at, :], acc_out.at[at, :], sems.at[n + 3 + i])

    @pl.loop(0, 4)
    def _(i):
        at = pl.ds(pl.multiple_of(i * 256, 256), 256)
        term = jnp.dot(yt[at, :], zz[...], preferred_element_type=F32)
        acc[at, :] = acc[at, :] + term if more else term
        store(i).start()

    @pl.loop(0, 4)
    def _(i):
        store(i).wait()


def early(bufs, left, right, acc=()):
    n = len(bufs)
    block = pltpu.VMEM((BLOCK, BLOCK), BF16)
    return pl.pallas_call(
        functools.partial(early_kernel, n, len(acc)),
        out_shape=pltpu.HBM((BLOCK, BLOCK), F32),
        in_specs=[ANY] * (n + 2 + len(acc)),
        out_specs=ANY,
        scratch_shapes=[
            pltpu.VMEM((BLOCK, n * TOK), BF16),
            pltpu.VMEM((n * TOK, BLOCK), BF16),
            pltpu.VMEM((n, TOK, 2 * BLOCK), BF16),
            block,
            block,
            pltpu.VMEM((BLOCK, BLOCK), F32),
            pltpu.SemaphoreType.DMA((n + 7,)),
        ],
        compiler_params=pltpu.CompilerParams(vmem_limit_bytes=20 << 20),
        cost_estimate=pl.CostEstimate(flops=6 * n * TOK * BLOCK * BLOCK, bytes_accessed=4 << 20, transcendentals=0),
        name="early",
    )(*[hbm(a) for a in (*bufs, left, right, *acc)])


def hold_kernel(gate, *refs):
    n = len(refs) // 2
    sources, outs, sems = refs[:n], refs[n : 2 * n], refs[2 * n]
    copies = [pltpu.make_async_copy(a, b, sems.at[i]) for i, (a, b) in enumerate(zip(sources, outs))]
    for copy in copies:
        copy.start()
    for copy in copies:
        copy.wait()


def hold(gate, arrays):
    return pl.pallas_call(
        hold_kernel,
        out_shape=[pltpu.VMEM(a.shape, a.dtype) for a in arrays],
        in_specs=[ANY] * (len(arrays) + 1),
        out_specs=[VM] * len(arrays),
        scratch_shapes=[pltpu.SemaphoreType.DMA((len(arrays),))],
        compiler_params=pltpu.CompilerParams(vmem_limit_bytes=1 << 20),
        cost_estimate=pl.CostEstimate(flops=0, bytes_accessed=8 << 20, transcendentals=0),
        name="hold",
    )(*[hbm(a) for a in (gate, *arrays)])


def final_kernel(n, *refs):
    (left, right, first, second), refs = refs[:4], refs[4:]
    operands, carried, refs = refs[: n + 1], refs[n + 1 : n + 5], refs[n + 5 :]
    (update, first_next, second_next), kept, refs = refs[:3], refs[3:7], refs[7:]
    held, yt, zz, direction, m_out, v_out, u_out, acc, sems, in_sems = refs
    places = [held.at[i] for i in range(n)] + [acc]
    pairs = [*zip(operands, places), *zip(carried, kept)]
    loads = [pltpu.make_async_copy(a, b, in_sems.at[i]) for i, (a, b) in enumerate(pairs)]
    for load in loads[: n + 1]:
        load.start()
    for load in loads[:n]:
        load.wait()
    rotate(places[:n], left, right, yt, zz)
    loads[n].wait()
    for load in loads[n + 1 :]:
        load.start()
    rows = 256

    def moment_copies(i):
        at = pl.ds(pl.multiple_of(i * rows, rows), rows)
        return (
            pltpu.make_async_copy(m_out.at[at, :], first_next.at[at, :], sems.at[i]),
            pltpu.make_async_copy(v_out.at[at, :], second_next.at[at, :], sems.at[4 + i]),
        )

    @pl.loop(0, BLOCK // rows, unroll=True)
    def _(i):
        at = pl.ds(pl.multiple_of(i * rows, rows), rows)
        rotated = acc[at, :] + jnp.dot(yt[at, :], zz[...], preferred_element_type=F32)
        share = 0.05 * rotated
        m = 0.95 * first[at, :].astype(F32) + share
        v = 0.95 * second[at, :].astype(F32) + share * rotated
        m_out[at, :] = m.astype(BF16)
        v_out[at, :] = v.astype(BF16)
        scaled = v * CORRECT
        root = scaled * lax.rsqrt(scaled) + CORRECT * 1e-08
        direction[at, :] = (m * pltpu.reciprocal(root, approx=True)).astype(BF16)
        for copy in moment_copies(i):
            copy.start()

    def update_copy(i):
        at = pl.ds(pl.multiple_of(i * 512, 512), 512)
        return pltpu.make_async_copy(u_out.at[at, :], update.at[at, :], sems.at[8 + i])

    @pl.loop(0, 2)
    def _(i):
        at = pl.ds(pl.multiple_of(i * 512, 512), 512)
        back = jnp.dot(left[at, :], direction[...], preferred_element_type=F32).astype(BF16)
        u_out[at, :] = lax.dot_general(
            back, right[...], (((1,), (1,)), ((), ())), preferred_element_type=F32
        ).astype(BF16)
        update_copy(i).start()

    @pl.loop(0, BLOCK // rows)
    def _(i):
        for copy in moment_copies(i):
            copy.wait()

    @pl.loop(0, 2)
    def _(i):
        update_copy(i).wait()

    for load in loads[n + 1 :]:
        load.wait()


def final(bufs, acc, left, right, first, second, carried):
    n = len(bufs)
    square = jax.ShapeDtypeStruct((BLOCK, BLOCK), BF16)
    block = pltpu.VMEM((BLOCK, BLOCK), BF16)
    return pl.pallas_call(
        functools.partial(final_kernel, n),
        out_shape=[square] * 3 + [pltpu.VMEM(a.shape, a.dtype) for a in carried],
        in_specs=[VM] * 4 + [ANY] * (n + 5),
        out_specs=[ANY] * 3 + [VM] * 4,
        scratch_shapes=[
            pltpu.VMEM((n, TOK, 2 * BLOCK), BF16),
            pltpu.VMEM((BLOCK, n * TOK), BF16),
            pltpu.VMEM((n * TOK, BLOCK), BF16),
            *[block] * 4,
            pltpu.VMEM((BLOCK, BLOCK), F32),
            pltpu.SemaphoreType.DMA((12,)),
            pltpu.SemaphoreType.DMA((n + 5,)),
        ],
        compiler_params=pltpu.CompilerParams(vmem_limit_bytes=28 << 20),
        cost_estimate=pl.CostEstimate(
            flops=(6 * n * TOK + 4 * BLOCK) * BLOCK * BLOCK, bytes_accessed=6 << 20, transcendentals=2 << 20
        ),
        name="final",
    )(
        *[vmem(a) for a in (left, right, first, second)],
        *[hbm(a) for a in (*bufs, acc, *carried)],
    )


def outer_kernel(half, total, params, momentum, snap, local, due, *rest):
    nexts, (params_out, momentum_out, local_out, sems) = rest[-7:-4], rest[-4:]

    def stores(i):
        at = pl.ds(pl.multiple_of((half[0] * 4 + i) * 16, 16), 16)
        mine = pl.ds(pl.multiple_of(i * 16, 16), 16)
        return [
            pltpu.make_async_copy(out.at[mine, :], to.at[at, :], sems.at[3 * i + k])
            for k, (out, to) in enumerate(zip((params_out, momentum_out, local_out), nexts))
        ]

    @pl.loop(0, 4)
    def _(i):
        at = pl.ds(pl.multiple_of((half[0] * 4 + i) * 16, 16), 16)
        mine = pl.ds(pl.multiple_of(i * 16, 16), 16)
        pseudo = total[mine, :].astype(F32) * (1.0 / 16)
        old, old_momentum = params[at, :], momentum[at, :]
        moment = 0.9 * old_momentum + pseudo
        stepped = old - 0.7 * (pseudo + 0.9 * moment)
        on = jnp.concatenate([due[at, :]] * (old.shape[1] // 128), axis=1) == 1
        params_out[mine, :] = jnp.where(on, stepped, old)
        momentum_out[mine, :] = jnp.where(on, moment, old_momentum)
        kept = local[at, :].astype(F32)
        local_out[mine, :] = jnp.where(on, stepped + (kept - snap[at, :].astype(F32)), kept).astype(BF16)
        for store in stores(i):
            store.start()

    @pl.loop(0, 4)
    def _(i):
        for store in stores(i):
            store.wait()


def outer(half, total, params, momentum, snap, local, due, into=()):
    rows, width = total.shape
    return pl.pallas_call(
        outer_kernel,
        out_shape=[
            pltpu.HBM(params.shape, F32),
            pltpu.HBM(params.shape, F32),
            pltpu.HBM(params.shape, BF16),
        ],
        in_specs=[pl.BlockSpec(memory_space=pltpu.SMEM)] + [VM] * 6 + [ANY] * len(into),
        out_specs=[ANY] * 3,
        scratch_shapes=[
            pltpu.VMEM((rows, width), F32),
            pltpu.VMEM((rows, width), F32),
            pltpu.VMEM((rows, width), BF16),
            pltpu.SemaphoreType.DMA((12,)),
        ],
        input_output_aliases={7 + i: i for i in range(len(into))},
        compiler_params=pltpu.CompilerParams(vmem_limit_bytes=16 << 20),
        cost_estimate=pl.CostEstimate(flops=5 << 20, bytes_accessed=12 << 20, transcendentals=0),
        name="outer",
    )(half[None], *[vmem(a) for a in (total, params, momentum, snap, local, due)], *into)


def after(array, others):
    return lax.optimization_barrier((array, *others))[0]


def added(one, two):
    return (one.astype(F32) + two.astype(F32)).astype(BF16)


def joined(mine, other, at):
    return lax.select(at == 0, jnp.concatenate([mine, other]), jnp.concatenate([other, mine]))


def per_device(
    tokens,
    out_grads,
    block_ids,
    left_basis,
    right_basis,
    first_moment,
    second_moment,
    outer_params,
    outer_momentum,
    snapshot,
    local_params,
    due_rows,
):
    replica = lax.axis_index("replica")
    y, core = replica // 4, replica % 2
    low, high = y % 2, y // 2
    at_a = jnp.where(core == 0, low ^ high, high)
    at_b = jnp.where(core == 0, high, low)

    def part(array, at):
        size = array.shape[0] // 2
        return lax.dynamic_slice_in_dim(array, at * size, size, 0)

    def difference(half):
        at = half * 64
        params = lax.dynamic_slice_in_dim(outer_params, at, 64, 0)
        return (params - lax.dynamic_slice_in_dim(snapshot[0], at, 64, 0).astype(F32)).astype(BF16)

    def along_y(pair, ids):
        quad = added(part(pair, at_a), to_y(part(pair, 1 - at_a), (1, 3)))
        rest = pick(ids, tokens, out_grads, (*SHIFTS[FIRST:], (0, 0)))
        return added(part(quad, at_b), to_y(part(quad, 1 - at_b), (3, 1))), *rest

    def no_along_y(pair, ids):
        return (pair[:16], *[pair[:32].reshape(-1, 2 * BLOCK)] * (len(SHIFTS) - FIRST + 1))

    def along_x(octet, sources):
        return added(octet, to_x(octet)), early(sources, left, right)

    def no_along_x(octet, sources):
        return octet, jnp.zeros((BLOCK, BLOCK), F32)

    def back(total, sources, acc):
        return joined(total, to_y(total, (3, 1)), at_b), early(sources, left, right, [acc])

    def no_back(total, sources, acc):
        return jnp.concatenate([total, total]), jnp.zeros((BLOCK, BLOCK), F32)

    always = replica >= 0
    left, right = left_basis[0, 0], right_basis[0, 0]
    pair = added(difference(core), to_core(difference(1 - core)))
    sends = pick(block_ids, tokens, out_grads, SHIFTS[:FIRST])
    got = [to_owner(a, dx, dz) for a, (dx, dz) in zip(sends, SHIFTS)]
    octet, *rest = lax.cond(always, along_y, no_along_y, after(pair, sends), block_ids)
    got += [to_owner(a, dx, dz) for a, (dx, dz) in zip(rest, SHIFTS[FIRST:])]
    total, acc = lax.cond(always, along_x, no_along_x, after(octet, got[:2]), [rest[-1], *got[:2]])
    rows, acc = lax.cond(always, back, no_back, after(total, got[2:EARLY]), got[2:EARLY], acc)
    left, right, first, second = hold(acc, (left, right, first_moment[0, 0], second_moment[0, 0]))
    rows = after(rows, [*got[EARLY:], left])
    rows = joined(rows, to_y(rows, (1, 3)), at_a)
    carried = (outer_params, outer_momentum, snapshot[0], local_params[0])
    update, first_next, second_next, *carried = final(
        got[EARLY:], acc, left, right, first, second, carried
    )
    rows = after(rows, [update])
    other = to_core(rows)
    due = jnp.broadcast_to(due_rows[:, None], (due_rows.shape[0], 128))
    state = (*carried, due)
    halves = outer(core, rows, *state)
    outer_next, momentum_next, local_next = outer(1 - core, other, *state, into=halves)
    return (
        update[None, None],
        first_next[None, None],
        second_next[None, None],
        outer_next,
        momentum_next,
        local_next[None],
    )


def solution(mesh):
    return jax.shard_map(
        per_device,
        mesh=mesh,
        in_specs=(
            P(("replica", "fsdp"), None),
            P(("replica", "fsdp"), None),
            P(),
            P("replica", "fsdp", None, None),
            P("replica", "fsdp", None, None),
            P("replica", "fsdp", None, None),
            P("replica", "fsdp", None, None),
            P("fsdp", None),
            P("fsdp", None),
            P("replica", "fsdp", None),
            P("replica", "fsdp", None),
            P("fsdp"),
        ),
        out_specs=(
            P("replica", "fsdp", None, None),
            P("replica", "fsdp", None, None),
            P("replica", "fsdp", None, None),
            P("fsdp", None),
            P("fsdp", None),
            P("replica", "fsdp", None),
        ),
        check_vma=False,
    )
```
